32 devices in a mesh: ctx: 16 (over z, y, x), tp: 2 (over core).
Axes of the slice: x: 2, y: 2, z: 4, core: 2. Of those that a mesh axis runs over, the one named last changes fastest.
Arguments:
- features: bfloat16 [3, 2048, 2048], P(None, 'tp', 'ctx'), may hold values from -6 to 6
- short_taps: float32 [7, 3, 2048], P(None, None, 'tp'), may hold values from -2.5 to 2.5
- long_filter: float32 [2048, 2048], P('tp', 'ctx'), may hold values from -0.125 to 0.125
- skip: float32 [2048], P('tp'), may hold values from 0.25 to 1.5
- norm_gain: float32 [2048], replicated, may hold values from 0.1 to 1.9
- w_qkv: bfloat16 [2048, 3, 2048], P('ctx', None, 'tp'), may hold values from -1 to 1
Outputs:
- mixed: bfloat16 [2048, 2048], P('tp', 'ctx')
- attended: bfloat16 [2048, 2048], P('ctx', 'tp')
The draws below stay inside these ranges and needn't reach their ends.
All inputs are finite; a program needn't handle non-finite values.
Results may differ from the reference program's by a relative error of at most 0.02.
Values may be sent and summed in bfloat16 or wider, within the bound.
A program may use at most 128 MiB of HBM per device.

```python
import jax
import jax.numpy as jnp
from jax import lax

C = 2048
H = 16
DH = 128
TAPS = 7
L = 2048


def draw_w_qkv(key, part):
    key = jax.random.fold_in(key, 11)
    first = jax.random.fold_in(key, 0)
    base = jax.random.normal(first, (C, 3, H * DH), jnp.float32) * C ** (-0.5)
    return jnp.clip(base, -1.0, 1.0).astype(jnp.bfloat16)


def block_levels(rng, shape, pieces, least, top_value):
    factor_of = 1.0
    for position, shards_of in pieces:
        draws = jax.random.uniform(jax.random.fold_in(jax.random.fold_in(rng, 6), position), (shards_of,), jnp.float32, least / len(pieces), top_value / len(pieces))
        factor_of = factor_of * jnp.repeat(jnp.exp(draws), shape[position] // shards_of).reshape((-1,) + (1,) * (len(shape) - 1 - position))
    return factor_of


def centred(own_key, dims, spread, limit, pieces=(), kind=jnp.bfloat16):
    loudness = block_levels(own_key, dims, pieces, -0.22, 0.18) if pieces else 1.0
    array = jax.random.normal(own_key, dims, jnp.float32) * spread * loudness
    return jnp.minimum(jnp.maximum(array, -limit), limit).astype(kind)


def setup_inputs(seed: int = 0) -> dict:
    streams_of = jax.random.split(jax.random.key(seed), 7)
    features = centred(streams_of[0], (3, C, L), 1.0, 6.0, ((1, 2), (2, 16)))
    short_taps = centred(streams_of[1], (TAPS, 3, C), 0.4, 2.5, ((2, 2),), jnp.float32)
    long_filter = centred(streams_of[2], (C, L), L ** -0.5, 0.125, ((0, 2), (1, 16)), jnp.float32)
    skip = jnp.clip(0.25 + 1.25 * jax.random.uniform(streams_of[3], (C,), jnp.float32) ** block_levels(streams_of[3], (C,), ((0, 2),), -0.2, 0.2), 0.25, 1.5)
    norm_gain = jnp.clip(1.0 + 0.18 * jax.random.normal(streams_of[4], (C,), jnp.float32), 0.1, 1.9)
    w_qkv = draw_w_qkv(jax.random.fold_in(streams_of[6], 71), 0)
    return dict(features=features, short_taps=short_taps, long_filter=long_filter, skip=skip, norm_gain=norm_gain, w_qkv=w_qkv)


def attention_head(parts):
    queries, keys, values = parts
    length = queries.shape[0]
    rows = min(1024, length)
    key_f = keys.astype(jnp.float32)
    value_f = values.astype(jnp.float32)
    key_pos = jnp.arange(length, dtype=jnp.int32)

    def one_block(index):
        start = (index * rows).astype(jnp.int32)
        block = lax.dynamic_slice_in_dim(queries, start, rows, 0).astype(jnp.float32)
        scores = jnp.dot(block, key_f.T) * DH ** (-0.5)
        query_pos = start + jnp.arange(rows, dtype=jnp.int32)
        allowed = key_pos[None, :] <= query_pos[:, None]
        scores = jnp.where(allowed, scores, -1e+30)
        top = lax.optimization_barrier(jnp.max(scores, axis=1, keepdims=True))
        expo = jnp.where(allowed, jnp.exp(scores - top), 0.0)
        total = lax.optimization_barrier(jnp.sum(expo, axis=1, keepdims=True))
        weights = lax.optimization_barrier(expo.astype(jnp.bfloat16)).astype(jnp.float32)
        return jnp.dot(weights, value_f) / total
    out = lax.map(one_block, jnp.arange(length // rows, dtype=jnp.int32))
    return out.reshape(length, -1)

def reference(features, short_taps, long_filter, skip, norm_gain, w_qkv):
    length = features.shape[2]
    values = features.astype(jnp.float32)
    padded = jnp.pad(values, ((0, 0), (0, 0), (TAPS - 1, 0)))
    short = short_taps[0][:, :, None] * padded[:, :, TAPS - 1:TAPS - 1 + length]
    for lag in range(1, TAPS):
        short = short + short_taps[lag][:, :, None] * padded[:, :, TAPS - 1 - lag:TAPS - 1 - lag + length]
    carried = (short[1] * short[2]).astype(jnp.bfloat16)
    lanes = carried.astype(jnp.float32)
    total = 2 * length
    spec = jnp.fft.rfft(lanes, n=total, axis=1) * jnp.fft.rfft(long_filter, n=total, axis=1)
    long_out = jnp.fft.irfft(spec, n=total, axis=1)[:, :length].astype(jnp.bfloat16)
    mixed = (short[0] * (long_out.astype(jnp.float32) + skip[:, None] * lanes)).astype(jnp.bfloat16)
    mixed_f = mixed.astype(jnp.float32)
    inverse = lax.rsqrt(lax.optimization_barrier(jnp.mean(mixed_f * mixed_f, axis=0, keepdims=True)) + 1e-06)
    normed = (mixed_f * inverse * norm_gain[:, None]).astype(jnp.bfloat16)
    weights = w_qkv.reshape(C, 3 * H * DH)
    projected = lax.dot_general(normed.astype(jnp.float32), weights.astype(jnp.float32), (((0,), (0,)), ((), ())), preferred_element_type=jnp.float32)
    projected = projected.astype(jnp.bfloat16).reshape(length, 3, H, DH)
    stacked = jnp.transpose(projected, (1, 2, 0, 3))
    heads_out = lax.map(attention_head, (stacked[0], stacked[1], stacked[2]))
    attended = jnp.transpose(heads_out, (1, 0, 2)).reshape(length, H * DH).astype(jnp.bfloat16)
    return (mixed, attended)
```

```python
import functools
import math

import jax
import jax.numpy as jnp
import ml_dtypes
import numpy as np
from jax import lax
from jax.experimental import pallas as pl
from jax.experimental.pallas import tpu as pltpu
from jax.sharding import PartitionSpec as P

DH = 128


HIGHEST = lax.Precision.HIGHEST


def shifted(block, axis, distance):
    devices = range(lax.axis_size(axis))
    route = [(i - distance, i) for i in devices if i - distance in devices]
    return lax.ppermute(block, axis, route)


def angle_table(rows, cols, modulus):
    left = jnp.arange(rows, dtype=jnp.int32)[:, None]
    right = jnp.arange(cols, dtype=jnp.int32)[None, :]
    phase = (left * right % modulus).astype(jnp.float32) * (2.0 * math.pi / modulus)
    return (jnp.cos(phase), jnp.sin(phase))


def contract(form, data, table):
    return jnp.einsum(form, data, table, precision=HIGHEST)


def spectrum(lanes, tok):
    width = lanes.shape[0]
    length = lanes.shape[1]
    outer = 2 * tok
    inner = 2 * length // outer
    data = lanes.reshape(width, tok, inner)
    cos_a, sin_a = angle_table(tok, outer, outer)
    first_re = contract("kaq,ab->kbq", data, cos_a)
    first_im = -contract("kaq,ab->kbq", data, sin_a)
    cos_t, sin_t = angle_table(outer, inner, 2 * length)
    turned_re = first_re * cos_t + first_im * sin_t
    turned_im = first_im * cos_t - first_re * sin_t
    cos_b, sin_b = angle_table(inner, inner, inner)
    out_re = contract("kbq,qr->kbr", turned_re, cos_b) + contract("kbq,qr->kbr", turned_im, sin_b)
    out_im = contract("kbq,qr->kbr", turned_im, cos_b) - contract("kbq,qr->kbr", turned_re, sin_b)
    return (out_re, out_im)


def inverse_real(spec_re, spec_im, tok, length):
    width = spec_re.shape[0]
    outer = 2 * tok
    inner = spec_re.shape[2]
    cos_b, sin_b = angle_table(inner, inner, inner)
    back_re = contract("kbr,rq->kbq", spec_re, cos_b) - contract("kbr,rq->kbq", spec_im, sin_b)
    back_im = contract("kbr,rq->kbq", spec_im, cos_b) + contract("kbr,rq->kbq", spec_re, sin_b)
    cos_t, sin_t = angle_table(outer, inner, 2 * length)
    turned_re = back_re * cos_t - back_im * sin_t
    turned_im = back_im * cos_t + back_re * sin_t
    cos_a, sin_a = angle_table(outer, tok, outer)
    real = contract("kbq,ba->kaq", turned_re, cos_a) - contract("kbq,ba->kaq", turned_im, sin_a)
    return (real / (2 * length)).reshape(width, length)


def attend_rows(query_rows, query_pos, keyvals, count, block):
    rows = query_rows.shape[0]
    scale = DH ** (-0.5)
    start_state = (
        jnp.full((rows,), -1e30, jnp.float32),
        jnp.zeros((rows,), jnp.float32),
        jnp.zeros((rows, DH), jnp.float32),
    )

    def step(index, state):
        running, total, accum = state
        part = lax.dynamic_slice_in_dim(keyvals, index * block, block, 0)
        keys = part[:, :DH]
        vals = part[:, DH:]
        scores = (
            lax.dot_general(
                query_rows, keys, (((1,), (1,)), ((), ())), preferred_element_type=jnp.float32
            )
            * scale
        )
        key_pos = index * block + jnp.arange(block, dtype=jnp.int32)
        allowed = key_pos[None, :] <= query_pos[:, None]
        scores = jnp.where(allowed, scores, -1e30)
        new_top = jnp.maximum(running, jnp.max(scores, axis=1))
        factor = jnp.exp(running - new_top)
        expo = jnp.where(allowed, jnp.exp(scores - new_top[:, None]), 0.0)
        total = total * factor + jnp.sum(expo, axis=1)
        accum = accum * factor[:, None] + jnp.dot(
            expo.astype(jnp.bfloat16), vals, preferred_element_type=jnp.float32
        )
        return (new_top, total, accum)

    running, total, accum = lax.fori_loop(0, count, step, start_state)
    return accum / total[:, None]


def local(features, short_taps, long_filter, skip, norm_gain, w_qkv):
    taps = short_taps.shape[0]
    tok = features.shape[2]
    rim = shifted(features[:, :, tok - (taps - 1) :], "ctx", 1)
    extended = jnp.concatenate([rim, features], axis=2).astype(jnp.float32)
    short = short_taps[0][:, :, None] * extended[:, :, taps - 1 : taps - 1 + tok]
    for lag in range(1, taps):
        short = (
            short
            + short_taps[lag][:, :, None] * extended[:, :, taps - 1 - lag : taps - 1 - lag + tok]
        )
    carried = (short[1] * short[2]).astype(jnp.bfloat16)
    lanes = lax.all_to_all(carried, "ctx", split_axis=0, concat_axis=1, tiled=True).astype(
        jnp.float32
    )
    filt = lax.all_to_all(long_filter, "ctx", split_axis=0, concat_axis=1, tiled=True)
    length = lanes.shape[1]
    data_re, data_im = spectrum(lanes, tok)
    filt_re, filt_im = spectrum(filt, tok)
    conv = inverse_real(
        data_re * filt_re - data_im * filt_im, data_re * filt_im + data_im * filt_re, tok, length
    )
    long_back = lax.all_to_all(
        conv.astype(jnp.bfloat16), "ctx", split_axis=1, concat_axis=0, tiled=True
    )
    mixed = (
        short[0] * (long_back.astype(jnp.float32) + skip[:, None] * carried.astype(jnp.float32))
    ).astype(jnp.bfloat16)
    whole = lax.all_gather(mixed, "tp", axis=0, tiled=True)
    whole_f = whole.astype(jnp.float32)
    inverse = lax.rsqrt(jnp.mean(whole_f * whole_f, axis=0, keepdims=True) + 1e-06)
    normed = (whole_f * inverse * norm_gain[:, None]).astype(jnp.bfloat16)
    columns = w_qkv.shape[1] * w_qkv.shape[2]
    piece = lax.all_gather(w_qkv, "ctx", axis=0, tiled=True)
    count = piece.shape[0]
    projected = lax.dot_general(
        normed,
        piece.reshape(count, columns),
        (((0,), (0,)), ((), ())),
        preferred_element_type=jnp.float32,
    )
    heads = w_qkv.shape[2] // DH
    projected = projected.astype(jnp.bfloat16).reshape(tok, 3, heads, DH)
    ranks = lax.axis_size("ctx")
    subs = ranks // heads
    sub = tok // subs
    key_pairs = jnp.concatenate([projected[:, 1], projected[:, 2]], axis=-1)
    slot = lax.axis_index("ctx") % subs
    queries = jnp.transpose(projected[:, 0].reshape(subs, sub, heads, DH), (2, 0, 1, 3)).reshape(
        ranks, sub, DH
    )
    pairs = jnp.transpose(key_pairs, (1, 0, 2))
    pairs = jnp.broadcast_to(pairs[:, None], (heads, subs, tok, 2 * DH)).reshape(ranks, tok, 2 * DH)
    got_queries = lax.all_to_all(queries, "ctx", split_axis=0, concat_axis=0, tiled=True).reshape(
        ranks * sub, DH
    )
    got_pairs = lax.all_to_all(pairs, "ctx", split_axis=0, concat_axis=0, tiled=True).reshape(
        ranks * tok, 2 * DH
    )
    source = jnp.arange(ranks * sub, dtype=jnp.int32)
    query_pos = source // sub * tok + slot * sub + source % sub
    total_keys = ranks * tok
    block = min(2048, total_keys)
    result = attend_rows(got_queries, query_pos, got_pairs, total_keys // block, block)
    result = result.astype(jnp.bfloat16).reshape(ranks, sub, DH)
    back = lax.all_to_all(result, "ctx", split_axis=0, concat_axis=0, tiled=True)
    attended = jnp.transpose(back.reshape(heads, subs, sub, DH), (1, 2, 0, 3)).reshape(
        tok, heads * DH
    )
    return (mixed, attended)


MESH = pl.DeviceIdType.MESH
F32 = jnp.float32
BF16 = jnp.bfloat16


def split_table(table):
    high = table.astype(ml_dtypes.bfloat16)
    low = (table - high.astype(np.float64)).astype(ml_dtypes.bfloat16)
    return jnp.asarray(high), jnp.asarray(low)


def packed_tables(tok):
    full = 2 * tok
    pos = np.arange(tok)[:, None]
    freq = np.arange(tok)[None, :]
    angle = 2.0 * np.pi * ((pos * freq) % full) / full
    imag = -np.sin(angle)
    imag[:, 0] = (-1.0) ** np.arange(tok)
    forward = np.concatenate([np.cos(angle), imag], axis=1)
    out = np.arange(full)[None, :]
    freq = np.arange(tok)[:, None]
    angle = 2.0 * np.pi * ((out * freq) % full) / full
    real = 2.0 * np.cos(angle)
    real[0] = 1.0
    imag = -2.0 * np.sin(angle)
    imag[0] = (-1.0) ** np.arange(full)
    backward = np.concatenate([real, imag], axis=0) / full
    return split_table(forward) + split_table(backward)


def hyena_kernel(
    dims,
    feats,
    filt,
    wts,
    coef,
    fwd_hi,
    fwd_lo,
    inv_hi,
    inv_lo,
    gathered,
    w_all,
    feat_all,
    filt_all,
    short0,
    carried,
    spec_x,
    spec_f,
    mixed,
    local_sem,
    feat_send,
    feat_recv,
    filt_send,
    filt_recv,
    w_send,
    w_recv,
    wx_send,
    wx_recv,
    x_send,
    x_recv,
    z_send,
    z_recv,
    y_send,
    y_recv,
    s_send,
    s_recv,
):
    ranks, nz, taps = dims
    me = lax.axis_index("ctx")
    core = lax.axis_index("tp")
    x = me % 2
    pair = me // 2
    y = pair % 2
    z = pair // 2
    width = filt_all.shape[1]
    tok = filt_all.shape[2]
    pairs = ranks // 2

    barrier = pltpu.get_barrier_semaphore()

    def greet(d, _):
        pl.semaphore_signal(
            barrier, inc=1, device_id=((me + d) % ranks, core), device_id_type=MESH
        )
        return 0

    lax.fori_loop(1, ranks, greet, 0)
    pl.semaphore_signal(barrier, inc=1, device_id=(me, 1 - core), device_id_type=MESH)
    pl.semaphore_wait(barrier, ranks)

    def remote(src, dst, send, recv, ctx, tp):
        return pltpu.make_async_remote_copy(
            src_ref=src, dst_ref=dst, send_sem=send, recv_sem=recv,
            device_id=(ctx, tp), device_id_type=MESH,
        )

    def feat_copy(d):
        to = (me + d) % ranks
        return remote(
            feats.at[:, pl.ds(to * width, width)], feat_all.at[me],
            feat_send.at[d], feat_recv.at[d], to, core,
        )

    def filt_copy(d):
        to = (me + d) % ranks
        return remote(
            filt.at[pl.ds(to * width, width)], filt_all.at[me],
            filt_send.at[d], filt_recv.at[d], to, core,
        )

    def w_copy(d):
        to = (pair + d) % pairs
        return remote(
            wts.at[to], w_all.at[pair, x], w_send.at[d], w_recv.at[d], to * 2 + x, core
        )

    own = [
        pltpu.make_async_copy(
            feats.at[:, pl.ds(me * width, width)], feat_all.at[me], local_sem.at[0]
        ),
        pltpu.make_async_copy(filt.at[pl.ds(me * width, width)], filt_all.at[me], local_sem.at[1]),
        pltpu.make_async_copy(wts.at[pair], w_all.at[pair, x], local_sem.at[2]),
    ]
    for copy in own:
        copy.start()
    for d in range(1, ranks):
        feat_copy(d).start()
    for d in range(1, ranks):
        filt_copy(d).start()
    for d in range(1, pairs):
        w_copy(d).start()
    own[0].wait()
    own[1].wait()
    for d in range(1, ranks):
        feat_copy(d).wait_recv()

    lane = lax.broadcasted_iota(jnp.int32, (width, tok), 1)
    first = lane == 0

    def short_block(b, _):
        before = jnp.maximum(b - 1, 0)
        live = jnp.where(b > 0, 1.0, 0.0).astype(F32)
        sums = []
        for i in range(3):
            now = feat_all[b, i].astype(F32)
            past = feat_all[before, i].astype(F32) * live
            total = coef[:, i : i + 1] * now
            for lag in range(1, taps):
                moved = jnp.where(
                    lane < lag, pltpu.roll(past, lag, 1), pltpu.roll(now, lag, 1)
                )
                total = total + coef[:, lag * 3 + i : lag * 3 + i + 1] * moved
            sums.append(total)
        short0[b] = sums[0]
        held = (sums[1] * sums[2]).astype(BF16)
        carried[b] = held
        spec_x[b] = jnp.dot(held, fwd_hi[...], preferred_element_type=F32) + jnp.dot(
            held, fwd_lo[...], preferred_element_type=F32
        )
        return 0

    lax.fori_loop(0, ranks, short_block, 0)
    for d in range(1, ranks):
        filt_copy(d).wait_recv()

    def filter_block(b, _):
        lags = filt_all[b]
        spec = jnp.dot(lags, fwd_hi[...], preferred_element_type=F32) + jnp.dot(
            lags, fwd_lo[...], preferred_element_type=F32
        )
        real = spec[:, :tok]
        imag = spec[:, tok:]
        spec_f[b, 0] = real
        spec_f[b, 1] = jnp.where(first, 0.0, imag)
        spec_f[b, 2] = jnp.where(first, imag, real)
        return 0

    lax.fori_loop(0, ranks, filter_block, 0)

    def block(m, tail):
        def term(d, acc):
            real, imag = acc
            xr = spec_x[m - d, :, :tok]
            xi = spec_x[m - d, :, tok:]
            f_re = spec_f[d, 0]
            f_im = spec_f[d, 1]
            f_ny = spec_f[d, 2]
            return (real + (xr * f_re - xi * f_im), imag + (xr * f_im + xi * f_ny))

        zero = jnp.zeros((width, tok), F32)
        real, imag = lax.fori_loop(0, m + 1, term, (zero, zero))
        spec = jnp.concatenate([real, imag], axis=1)
        high = spec.astype(BF16)
        low = (spec - high.astype(F32)).astype(BF16)
        wave = (
            jnp.dot(high, inv_hi[...], preferred_element_type=F32)
            + jnp.dot(low, inv_hi[...], preferred_element_type=F32)
            + jnp.dot(high, inv_lo[...], preferred_element_type=F32)
        )
        long_out = (wave[:, :tok] + tail).astype(BF16).astype(F32)
        skip = coef[:, 3 * taps : 3 * taps + 1]
        value = short0[m] * (long_out + skip * carried[m].astype(F32))
        mixed[m % 2, :, pl.ds(pl.multiple_of((m // 2) * tok, tok), tok)] = value.astype(BF16)
        return wave[:, tok:]

    lax.fori_loop(0, ranks, block, jnp.zeros((width, tok), F32))

    keep = pltpu.make_async_copy(mixed.at[x], gathered.at[core, pair, x], local_sem.at[3])
    keep.start()
    swap = remote(
        mixed.at[1 - x], gathered.at[core, pair, x], x_send.at[0], x_recv.at[0],
        pair * 2 + 1 - x, core,
    )
    swap.start()
    keep.wait()
    swap.wait_recv()

    def chunk(p):
        return gathered.at[core, p]

    def z_copy(d):
        to = (z + d) % nz
        return remote(
            chunk(pair), chunk(pair), z_send.at[d], z_recv.at[d], to * 4 + y * 2 + x, core
        )

    def y_copy(d):
        p = ((z - d + nz) % nz) * 2 + y
        return remote(
            chunk(p), chunk(p), y_send.at[d], y_recv.at[d], z * 4 + (1 - y) * 2 + x, core
        )

    def s_copy(d, side):
        p = ((z - d + nz) % nz) * 2 + jnp.where(side == 0, y, 1 - y)
        return remote(
            chunk(p), chunk(p), s_send.at[side * nz + d], s_recv.at[side * nz + d], me, 1 - core
        )

    y_copy(0).start()
    for d in range(1, nz):
        z_copy(d).start()
    s_copy(0, 0).start()

    own[2].wait()
    for d in range(1, pairs):
        w_copy(d).wait_recv()
    w_swap = remote(
        w_all.at[:, x], w_all.at[:, x], wx_send.at[0], wx_recv.at[0], pair * 2 + 1 - x, core
    )
    w_swap.start()

    for d in range(1, nz):
        z_copy(d).wait_recv()
        y_copy(d).start()
        s_copy(d, 0).start()
    for d in range(nz):
        y_copy(d).wait_recv()
        s_copy(d, 1).start()
    for d in range(nz):
        s_copy(d, 0).wait_recv()
        s_copy(d, 1).wait_recv()
    w_swap.wait()
    for d in range(1, ranks):
        feat_copy(d).wait_send()
        filt_copy(d).wait_send()
    for d in range(1, pairs):
        w_copy(d).wait_send()
    swap.wait_send()
    for d in range(1, nz):
        z_copy(d).wait_send()
    for d in range(nz):
        y_copy(d).wait_send()
        s_copy(d, 0).wait_send()
        s_copy(d, 1).wait_send()


def hyena(features, filt, wts, coef, nz, taps):
    ranks = features.shape[1] // coef.shape[0]
    width = coef.shape[0]
    tok = features.shape[2]
    pairs = ranks // 2
    rows, columns = wts.shape[1:]
    tables = packed_tables(tok)
    vmem = pl.BlockSpec(memory_space=pltpu.VMEM)
    hbm = pl.BlockSpec(memory_space=pl.ANY)
    dma = pltpu.SemaphoreType.DMA
    return pl.pallas_call(
        functools.partial(hyena_kernel, (ranks, nz, taps)),
        out_shape=(
            jax.ShapeDtypeStruct((2, pairs, 2, width, pairs * tok), BF16),
            jax.ShapeDtypeStruct((pairs, 2, rows, columns), BF16),
        ),
        in_specs=[hbm, hbm, hbm] + [vmem] * 5,
        out_specs=(hbm, hbm),
        scratch_shapes=[
            pltpu.VMEM((ranks, 3, width, tok), BF16),
            pltpu.VMEM((ranks, width, tok), BF16),
            pltpu.VMEM((ranks, width, tok), F32),
            pltpu.VMEM((ranks, width, tok), BF16),
            pltpu.VMEM((ranks, width, 2 * tok), F32),
            pltpu.VMEM((ranks, 3, width, tok), F32),
            pltpu.VMEM((2, width, pairs * tok), BF16),
            dma((4,)),
            dma((ranks,)),
            dma((ranks,)),
            dma((ranks,)),
            dma((ranks,)),
            dma((pairs,)),
            dma((pairs,)),
            dma((1,)),
            dma((1,)),
            dma((1,)),
            dma((1,)),
            dma((nz,)),
            dma((nz,)),
            dma((nz,)),
            dma((nz,)),
            dma((2 * nz,)),
            dma((2 * nz,)),
        ],
        compiler_params=pltpu.CompilerParams(
            collective_id=0, has_side_effects=True, vmem_limit_bytes=32 * 2**20
        ),
    )(features, filt, wts, coef, *tables)


def return_kernel(pairs, result, out, local_sem, send, recv):
    me = lax.axis_index("ctx")
    core = lax.axis_index("tp")
    x = me % 2
    pair = me // 2
    barrier = pltpu.get_barrier_semaphore()
    for d in range(1, pairs):
        to = (pair + d) % pairs
        pl.semaphore_signal(barrier, inc=1, device_id=(to * 2 + x, core), device_id_type=MESH)
    pl.semaphore_wait(barrier, pairs - 1)
    own = pltpu.make_async_copy(result.at[pair], out.at[pair], local_sem)
    own.start()

    def copy(d):
        to = (pair + d) % pairs
        return pltpu.make_async_remote_copy(
            src_ref=result.at[to], dst_ref=out.at[pair], send_sem=send.at[d],
            recv_sem=recv.at[d], device_id=(to * 2 + x, core), device_id_type=MESH,
        )

    for d in range(1, pairs):
        copy(d).start()
    own.wait()
    for d in range(1, pairs):
        copy(d).wait()


def give_back(result):
    pairs = result.shape[0]
    hbm = pl.BlockSpec(memory_space=pltpu.VMEM)
    return pl.pallas_call(
        functools.partial(return_kernel, pairs),
        out_shape=jax.ShapeDtypeStruct(result.shape, result.dtype),
        in_specs=[hbm],
        out_specs=hbm,
        scratch_shapes=[
            pltpu.SemaphoreType.DMA,
            pltpu.SemaphoreType.DMA((pairs,)),
            pltpu.SemaphoreType.DMA((pairs,)),
        ],
        compiler_params=pltpu.CompilerParams(collective_id=1, has_side_effects=True),
    )(result)


def local_pairs(features, short_taps, long_filter, skip, norm_gain, w_qkv):
    ranks = lax.axis_size("ctx")
    pairs = ranks // 2
    me = lax.axis_index("ctx")
    core = lax.axis_index("tp")
    x = me % 2
    taps = short_taps.shape[0]
    tok = features.shape[2]
    width = features.shape[1] // ranks
    coef = jnp.concatenate([short_taps.reshape(taps * 3, -1), skip[None]], axis=0)
    coef = lax.dynamic_slice_in_dim(coef, me * width, width, 1).T
    rows = w_qkv.shape[0]
    wts = jnp.transpose(w_qkv.reshape(rows, 3, pairs, DH), (2, 0, 1, 3)).reshape(
        pairs, rows, 3 * DH
    )
    gathered, w_all = hyena(
        features, long_filter.astype(BF16), wts, coef, ranks // 4, taps
    )
    channels = norm_gain.shape[0]
    whole = gathered.reshape(channels, pairs * tok)
    half = lax.dynamic_slice(
        whole, (core * (channels // 2), (me // 2) * tok), (channels // 2, tok)
    )
    whole_f = whole.astype(F32)
    inverse = lax.rsqrt(jnp.mean(whole_f * whole_f, axis=0, keepdims=True) + 1e-06)
    normed = (whole_f * inverse * norm_gain[:, None]).astype(BF16)
    projected = lax.dot_general(
        normed, w_all.reshape(channels, 3 * DH), (((0,), (0,)), ((), ())),
        preferred_element_type=F32,
    ).astype(BF16)
    mine = projected[:, DH:]
    other = lax.ppermute(mine, "ctx", [(i, i ^ 1) for i in range(ranks)])
    mine = mine.reshape(pairs, 1, tok, 2 * DH)
    other = other.reshape(pairs, 1, tok, 2 * DH)
    even = jnp.where(x == 0, mine, other)
    odd = jnp.where(x == 0, other, mine)
    keyvals = jnp.concatenate([even, odd], axis=1).reshape(ranks * tok, 2 * DH)
    source = jnp.arange(pairs * tok, dtype=jnp.int32)
    query_pos = (source // tok * 2 + x) * tok + source % tok
    result = attend_rows(projected[:, :DH], query_pos, keyvals, 1, ranks * tok)
    back = give_back(result.astype(BF16).reshape(pairs, tok, DH))
    attended = jnp.transpose(back, (1, 0, 2)).reshape(tok, pairs * DH)
    return (half, attended)


def solution(mesh):
    in_specs = (
        P(None, "tp", "ctx"),
        P(None, None, "tp"),
        P("tp", "ctx"),
        P("tp"),
        P(),
        P("ctx", None, "tp"),
    )
    out_specs = (P("tp", "ctx"), P("ctx", "tp"))

    def whole(features, short_taps, long_filter, skip, norm_gain, w_qkv):
        heads = w_qkv.shape[2] // mesh.shape["tp"] // DH
        paired = mesh.shape["ctx"] == 16 and heads == 8
        body = local_pairs if paired else local
        return jax.shard_map(
            body, mesh=mesh, in_specs=in_specs, out_specs=out_specs, check_vma=False
        )(features, short_taps, long_filter, skip, norm_gain, w_qkv)

    return whole
```

```python
import functools
import math

import jax
import jax.numpy as jnp
import ml_dtypes
import numpy as np
from jax import lax
from jax.experimental import pallas as pl
from jax.experimental.pallas import tpu as pltpu
from jax.sharding import PartitionSpec as P

DH = 128


HIGHEST = lax.Precision.HIGHEST


def shifted(block, axis, distance):
    devices = range(lax.axis_size(axis))
    route = [(i - distance, i) for i in devices if i - distance in devices]
    return lax.ppermute(block, axis, route)


def angle_table(rows, cols, modulus):
    left = jnp.arange(rows, dtype=jnp.int32)[:, None]
    right = jnp.arange(cols, dtype=jnp.int32)[None, :]
    phase = (left * right % modulus).astype(jnp.float32) * (2.0 * math.pi / modulus)
    return (jnp.cos(phase), jnp.sin(phase))


def contract(form, data, table):
    return jnp.einsum(form, data, table, precision=HIGHEST)


def spectrum(lanes, tok):
    width = lanes.shape[0]
    length = lanes.shape[1]
    outer = 2 * tok
    inner = 2 * length // outer
    data = lanes.reshape(width, tok, inner)
    cos_a, sin_a = angle_table(tok, outer, outer)
    first_re = contract("kaq,ab->kbq", data, cos_a)
    first_im = -contract("kaq,ab->kbq", data, sin_a)
    cos_t, sin_t = angle_table(outer, inner, 2 * length)
    turned_re = first_re * cos_t + first_im * sin_t
    turned_im = first_im * cos_t - first_re * sin_t
    cos_b, sin_b = angle_table(inner, inner, inner)
    out_re = contract("kbq,qr->kbr", turned_re, cos_b) + contract("kbq,qr->kbr", turned_im, sin_b)
    out_im = contract("kbq,qr->kbr", turned_im, cos_b) - contract("kbq,qr->kbr", turned_re, sin_b)
    return (out_re, out_im)


def inverse_real(spec_re, spec_im, tok, length):
    width = spec_re.shape[0]
    outer = 2 * tok
    inner = spec_re.shape[2]
    cos_b, sin_b = angle_table(inner, inner, inner)
    back_re = contract("kbr,rq->kbq", spec_re, cos_b) - contract("kbr,rq->kbq", spec_im, sin_b)
    back_im = contract("kbr,rq->kbq", spec_im, cos_b) + contract("kbr,rq->kbq", spec_re, sin_b)
    cos_t, sin_t = angle_table(outer, inner, 2 * length)
    turned_re = back_re * cos_t - back_im * sin_t
    turned_im = back_im * cos_t + back_re * sin_t
    cos_a, sin_a = angle_table(outer, tok, outer)
    real = contract("kbq,ba->kaq", turned_re, cos_a) - contract("kbq,ba->kaq", turned_im, sin_a)
    return (real / (2 * length)).reshape(width, length)


def attend_rows(query_rows, query_pos, keyvals, count, block):
    rows = query_rows.shape[0]
    scale = DH ** (-0.5)
    start_state = (
        jnp.full((rows,), -1e30, jnp.float32),
        jnp.zeros((rows,), jnp.float32),
        jnp.zeros((rows, DH), jnp.float32),
    )

    def step(index, state):
        running, total, accum = state
        part = lax.dynamic_slice_in_dim(keyvals, index * block, block, 0)
        keys = part[:, :DH]
        vals = part[:, DH:]
        scores = (
            lax.dot_general(
                query_rows, keys, (((1,), (1,)), ((), ())), preferred_element_type=jnp.float32
            )
            * scale
        )
        key_pos = index * block + jnp.arange(block, dtype=jnp.int32)
        allowed = key_pos[None, :] <= query_pos[:, None]
        scores = jnp.where(allowed, scores, -1e30)
        new_top = jnp.maximum(running, jnp.max(scores, axis=1))
        factor = jnp.exp(running - new_top)
        expo = jnp.where(allowed, jnp.exp(scores - new_top[:, None]), 0.0)
        total = total * factor + jnp.sum(expo, axis=1)
        accum = accum * factor[:, None] + jnp.dot(
            expo.astype(jnp.bfloat16), vals, preferred_element_type=jnp.float32
        )
        return (new_top, total, accum)

    running, total, accum = lax.fori_loop(0, count, step, start_state)
    return accum / total[:, None]


def local(features, short_taps, long_filter, skip, norm_gain, w_qkv):
    taps = short_taps.shape[0]
    tok = features.shape[2]
    rim = shifted(features[:, :, tok - (taps - 1) :], "ctx", 1)
    extended = jnp.concatenate([rim, features], axis=2).astype(jnp.float32)
    short = short_taps[0][:, :, None] * extended[:, :, taps - 1 : taps - 1 + tok]
    for lag in range(1, taps):
        short = (
            short
            + short_taps[lag][:, :, None] * extended[:, :, taps - 1 - lag : taps - 1 - lag + tok]
        )
    carried = (short[1] * short[2]).astype(jnp.bfloat16)
    lanes = lax.all_to_all(carried, "ctx", split_axis=0, concat_axis=1, tiled=True).astype(
        jnp.float32
    )
    filt = lax.all_to_all(long_filter, "ctx", split_axis=0, concat_axis=1, tiled=True)
    length = lanes.shape[1]
    data_re, data_im = spectrum(lanes, tok)
    filt_re, filt_im = spectrum(filt, tok)
    conv = inverse_real(
        data_re * filt_re - data_im * filt_im, data_re * filt_im + data_im * filt_re, tok, length
    )
    long_back = lax.all_to_all(
        conv.astype(jnp.bfloat16), "ctx", split_axis=1, concat_axis=0, tiled=True
    )
    mixed = (
        short[0] * (long_back.astype(jnp.float32) + skip[:, None] * carried.astype(jnp.float32))
    ).astype(jnp.bfloat16)
    whole = lax.all_gather(mixed, "tp", axis=0, tiled=True)
    whole_f = whole.astype(jnp.float32)
    inverse = lax.rsqrt(jnp.mean(whole_f * whole_f, axis=0, keepdims=True) + 1e-06)
    normed = (whole_f * inverse * norm_gain[:, None]).astype(jnp.bfloat16)
    columns = w_qkv.shape[1] * w_qkv.shape[2]
    piece = lax.all_gather(w_qkv, "ctx", axis=0, tiled=True)
    count = piece.shape[0]
    projected = lax.dot_general(
        normed,
        piece.reshape(count, columns),
        (((0,), (0,)), ((), ())),
        preferred_element_type=jnp.float32,
    )
    heads = w_qkv.shape[2] // DH
    projected = projected.astype(jnp.bfloat16).reshape(tok, 3, heads, DH)
    ranks = lax.axis_size("ctx")
    subs = ranks // heads
    sub = tok // subs
    key_pairs = jnp.concatenate([projected[:, 1], projected[:, 2]], axis=-1)
    slot = lax.axis_index("ctx") % subs
    queries = jnp.transpose(projected[:, 0].reshape(subs, sub, heads, DH), (2, 0, 1, 3)).reshape(
        ranks, sub, DH
    )
    pairs = jnp.transpose(key_pairs, (1, 0, 2))
    pairs = jnp.broadcast_to(pairs[:, None], (heads, subs, tok, 2 * DH)).reshape(ranks, tok, 2 * DH)
    got_queries = lax.all_to_all(queries, "ctx", split_axis=0, concat_axis=0, tiled=True).reshape(
        ranks * sub, DH
    )
    got_pairs = lax.all_to_all(pairs, "ctx", split_axis=0, concat_axis=0, tiled=True).reshape(
        ranks * tok, 2 * DH
    )
    source = jnp.arange(ranks * sub, dtype=jnp.int32)
    query_pos = source // sub * tok + slot * sub + source % sub
    total_keys = ranks * tok
    block = min(2048, total_keys)
    result = attend_rows(got_queries, query_pos, got_pairs, total_keys // block, block)
    result = result.astype(jnp.bfloat16).reshape(ranks, sub, DH)
    back = lax.all_to_all(result, "ctx", split_axis=0, concat_axis=0, tiled=True)
    attended = jnp.transpose(back.reshape(heads, subs, sub, DH), (1, 2, 0, 3)).reshape(
        tok, heads * DH
    )
    return (mixed, attended)


MESH = pl.DeviceIdType.MESH
F32 = jnp.float32
BF16 = jnp.bfloat16


def split_table(table):
    high = table.astype(ml_dtypes.bfloat16)
    low = (table - high.astype(np.float64)).astype(ml_dtypes.bfloat16)
    return jnp.asarray(high), jnp.asarray(low)


def packed_tables(tok):
    full = 2 * tok
    pos = np.arange(tok)[:, None]
    freq = np.arange(tok)[None, :]
    angle = 2.0 * np.pi * ((pos * freq) % full) / full
    imag = -np.sin(angle)
    imag[:, 0] = (-1.0) ** np.arange(tok)
    forward = np.concatenate([np.cos(angle), imag], axis=1)
    out = np.arange(full)[None, :]
    freq = np.arange(tok)[:, None]
    angle = 2.0 * np.pi * ((out * freq) % full) / full
    real = 2.0 * np.cos(angle)
    real[0] = 1.0
    imag = -2.0 * np.sin(angle)
    imag[0] = (-1.0) ** np.arange(full)
    backward = np.concatenate([real, imag], axis=0) / full
    return split_table(forward) + split_table(backward)


def hyena_kernel(
    dims,
    feats,
    filt_in,
    w_in,
    coef_in,
    fwd_hi_in,
    fwd_lo_in,
    inv_hi_in,
    inv_lo_in,
    gathered,
    w_all,
    filt_wide,
    filt,
    w_raw,
    wts,
    coef,
    fwd_hi,
    fwd_lo,
    inv_hi,
    inv_lo,
    feat_all,
    filt_all,
    short0,
    carried,
    spec_x,
    spec_f,
    mixed,
    local_sem,
    feat_send,
    feat_recv,
    filt_send,
    filt_recv,
    w_send,
    w_recv,
    wx_send,
    wx_recv,
    x_send,
    x_recv,
    z_send,
    z_recv,
    y_send,
    y_recv,
    s_send,
    s_recv,
):
    ranks, nz, taps = dims
    me = lax.axis_index("ctx")
    core = lax.axis_index("tp")
    x = me % 2
    pair = me // 2
    y = pair % 2
    z = pair // 2
    width = filt_all.shape[1]
    tok = filt_all.shape[2]
    pairs = ranks // 2

    barrier = pltpu.get_barrier_semaphore()

    def greet(d, _):
        pl.semaphore_signal(
            barrier, inc=1, device_id=((me + d) % ranks, core), device_id_type=MESH
        )
        return 0

    lax.fori_loop(1, ranks, greet, 0)
    pl.semaphore_signal(barrier, inc=1, device_id=(me, 1 - core), device_id_type=MESH)
    pl.semaphore_wait(barrier, ranks)

    def remote(src, dst, send, recv, ctx, tp):
        return pltpu.make_async_remote_copy(
            src_ref=src, dst_ref=dst, send_sem=send, recv_sem=recv,
            device_id=(ctx, tp), device_id_type=MESH,
        )

    def feat_copy(d):
        to = (me + d) % ranks
        return remote(
            feats.at[:, pl.ds(to * width, width)], feat_all.at[me],
            feat_send.at[d], feat_recv.at[d], to, core,
        )

    def filt_copy(d):
        to = (me + d) % ranks
        return remote(
            filt.at[pl.ds(to * width, width)], filt_all.at[me],
            filt_send.at[d], filt_recv.at[d], to, core,
        )

    def w_copy(d):
        to = (pair + d) % pairs
        return remote(
            wts.at[to], w_all.at[pair, x], w_send.at[d], w_recv.at[d], to * 2 + x, core
        )

    loads = [
        pltpu.make_async_copy(src, dst, local_sem.at[4 + i])
        for i, (src, dst) in enumerate(
            (
                (filt_in, filt_wide),
                (w_in, w_raw),
                (coef_in, coef),
                (fwd_hi_in, fwd_hi),
                (fwd_lo_in, fwd_lo),
                (inv_hi_in, inv_hi),
                (inv_lo_in, inv_lo),
            )
        )
    ]
    for d in range(1, ranks):
        feat_copy(d).start()
    for load in loads:
        load.start()
    own = [
        pltpu.make_async_copy(
            feats.at[:, pl.ds(me * width, width)], feat_all.at[me], local_sem.at[0]
        ),
        pltpu.make_async_copy(filt.at[pl.ds(me * width, width)], filt_all.at[me], local_sem.at[1]),
        pltpu.make_async_copy(wts.at[pair], w_all.at[pair, x], local_sem.at[2]),
    ]
    own[0].start()
    loads[0].wait()
    filt[...] = filt_wide[...].astype(BF16)
    own[1].start()
    for d in range(1, ranks):
        filt_copy(d).start()
    loads[1].wait()
    for i in range(3):
        for h in range(pairs):
            wts[h, :, i * DH : (i + 1) * DH] = w_raw[:, i, h * DH : (h + 1) * DH]
    own[2].start()
    for load in loads[2:]:
        load.wait()
    own[0].wait()
    own[1].wait()
    for d in range(1, ranks):
        feat_copy(d).wait_recv()
    for d in range(1, pairs):
        w_copy(d).start()

    lane = lax.broadcasted_iota(jnp.int32, (width, tok), 1)
    first = lane == 0

    def short_block(b, _):
        before = jnp.maximum(b - 1, 0)
        live = jnp.where(b > 0, 1.0, 0.0).astype(F32)
        sums = []
        for i in range(3):
            now = feat_all[b, i].astype(F32)
            past = feat_all[before, i].astype(F32) * live
            total = coef[:, i : i + 1] * now
            for lag in range(1, taps):
                moved = jnp.where(
                    lane < lag, pltpu.roll(past, lag, 1), pltpu.roll(now, lag, 1)
                )
                total = total + coef[:, lag * 3 + i : lag * 3 + i + 1] * moved
            sums.append(total)
        short0[b] = sums[0]
        held = (sums[1] * sums[2]).astype(BF16)
        carried[b] = held
        spec_x[b] = jnp.dot(held, fwd_hi[...], preferred_element_type=F32) + jnp.dot(
            held, fwd_lo[...], preferred_element_type=F32
        )
        return 0

    lax.fori_loop(0, ranks, short_block, 0)
    for d in range(1, ranks):
        filt_copy(d).wait_recv()

    def filter_block(b, _):
        lags = filt_all[b]
        spec = jnp.dot(lags, fwd_hi[...], preferred_element_type=F32) + jnp.dot(
            lags, fwd_lo[...], preferred_element_type=F32
        )
        real = spec[:, :tok]
        imag = spec[:, tok:]
        spec_f[b, 0] = real
        spec_f[b, 1] = jnp.where(first, 0.0, imag)
        spec_f[b, 2] = jnp.where(first, imag, real)
        return 0

    lax.fori_loop(0, ranks, filter_block, 0)

    def block(m, tail):
        def term(d, acc):
            real, imag = acc
            xr = spec_x[m - d, :, :tok]
            xi = spec_x[m - d, :, tok:]
            f_re = spec_f[d, 0]
            f_im = spec_f[d, 1]
            f_ny = spec_f[d, 2]
            return (real + (xr * f_re - xi * f_im), imag + (xr * f_im + xi * f_ny))

        zero = jnp.zeros((width, tok), F32)
        real, imag = lax.fori_loop(0, m + 1, term, (zero, zero))
        spec = jnp.concatenate([real, imag], axis=1)
        high = spec.astype(BF16)
        low = (spec - high.astype(F32)).astype(BF16)
        wave = (
            jnp.dot(high, inv_hi[...], preferred_element_type=F32)
            + jnp.dot(low, inv_hi[...], preferred_element_type=F32)
            + jnp.dot(high, inv_lo[...], preferred_element_type=F32)
        )
        long_out = (wave[:, :tok] + tail).astype(BF16).astype(F32)
        skip = coef[:, 3 * taps : 3 * taps + 1]
        value = short0[m] * (long_out + skip * carried[m].astype(F32))
        mixed[m % 2, :, pl.ds(pl.multiple_of((m // 2) * tok, tok), tok)] = value.astype(BF16)
        return wave[:, tok:]

    lax.fori_loop(0, ranks, block, jnp.zeros((width, tok), F32))

    keep = pltpu.make_async_copy(mixed.at[x], gathered.at[core, pair, x], local_sem.at[3])
    keep.start()
    swap = remote(
        mixed.at[1 - x], gathered.at[core, pair, x], x_send.at[0], x_recv.at[0],
        pair * 2 + 1 - x, core,
    )
    swap.start()
    keep.wait()
    swap.wait_recv()

    def chunk(p):
        return gathered.at[core, p]

    def z_copy(d):
        to = (z + d) % nz
        return remote(
            chunk(pair), chunk(pair), z_send.at[d], z_recv.at[d], to * 4 + y * 2 + x, core
        )

    def y_copy(d):
        p = ((z - d + nz) % nz) * 2 + y
        return remote(
            chunk(p), chunk(p), y_send.at[d], y_recv.at[d], z * 4 + (1 - y) * 2 + x, core
        )

    def s_copy(d, side):
        p = ((z - d + nz) % nz) * 2 + jnp.where(side == 0, y, 1 - y)
        return remote(
            chunk(p), chunk(p), s_send.at[side * nz + d], s_recv.at[side * nz + d], me, 1 - core
        )

    y_copy(0).start()
    for d in range(1, nz):
        z_copy(d).start()
    s_copy(0, 0).start()

    own[2].wait()
    for d in range(1, pairs):
        w_copy(d).wait_recv()
    w_swap = remote(
        w_all.at[:, x], w_all.at[:, x], wx_send.at[0], wx_recv.at[0], pair * 2 + 1 - x, core
    )
    w_swap.start()

    for d in range(1, nz):
        z_copy(d).wait_recv()
        y_copy(d).start()
        s_copy(d, 0).start()
    for d in range(nz):
        y_copy(d).wait_recv()
        s_copy(d, 1).start()
    for d in range(nz):
        s_copy(d, 0).wait_recv()
        s_copy(d, 1).wait_recv()
    w_swap.wait()
    for d in range(1, ranks):
        feat_copy(d).wait_send()
        filt_copy(d).wait_send()
    for d in range(1, pairs):
        w_copy(d).wait_send()
    swap.wait_send()
    for d in range(1, nz):
        z_copy(d).wait_send()
    for d in range(nz):
        y_copy(d).wait_send()
        s_copy(d, 0).wait_send()
        s_copy(d, 1).wait_send()


def hyena(features, filt, w_qkv, coef, nz, taps):
    ranks = features.shape[1] // coef.shape[0]
    width = coef.shape[0]
    tok = features.shape[2]
    pairs = ranks // 2
    rows = w_qkv.shape[0]
    columns = 3 * DH
    tables = packed_tables(tok)
    hbm = pl.BlockSpec(memory_space=pl.ANY)
    dma = pltpu.SemaphoreType.DMA
    return pl.pallas_call(
        functools.partial(hyena_kernel, (ranks, nz, taps)),
        out_shape=(
            jax.ShapeDtypeStruct((2, pairs, 2, width, pairs * tok), BF16),
            jax.ShapeDtypeStruct((pairs, 2, rows, columns), BF16),
        ),
        in_specs=[hbm] * 8,
        out_specs=(hbm, hbm),
        scratch_shapes=[
            pltpu.VMEM(filt.shape, F32),
            pltpu.VMEM(filt.shape, BF16),
            pltpu.VMEM(w_qkv.shape, BF16),
            pltpu.VMEM((pairs, rows, columns), BF16),
            pltpu.VMEM(coef.shape, F32),
        ]
        + [pltpu.VMEM(table.shape, BF16) for table in tables]
        + [
            pltpu.VMEM((ranks, 3, width, tok), BF16),
            pltpu.VMEM((ranks, width, tok), BF16),
            pltpu.VMEM((ranks, width, tok), F32),
            pltpu.VMEM((ranks, width, tok), BF16),
            pltpu.VMEM((ranks, width, 2 * tok), F32),
            pltpu.VMEM((ranks, 3, width, tok), F32),
            pltpu.VMEM((2, width, pairs * tok), BF16),
            dma((11,)),
            dma((ranks,)),
            dma((ranks,)),
            dma((ranks,)),
            dma((ranks,)),
            dma((pairs,)),
            dma((pairs,)),
            dma((1,)),
            dma((1,)),
            dma((1,)),
            dma((1,)),
            dma((nz,)),
            dma((nz,)),
            dma((nz,)),
            dma((nz,)),
            dma((2 * nz,)),
            dma((2 * nz,)),
        ],
        compiler_params=pltpu.CompilerParams(
            collective_id=0, has_side_effects=True, vmem_limit_bytes=32 * 2**20
        ),
    )(features, filt, w_qkv, coef, *tables)


def attend_kernel(
    pairs, tok, proj, out, other, top, total, accum, result,
    local_sem, kv_send, kv_recv, send, recv,
):
    me = lax.axis_index("ctx")
    core = lax.axis_index("tp")
    x = me % 2
    pair = me // 2
    parts = kv_send.shape[0]
    rows = pairs * tok // parts
    scale = DH ** (-0.5)

    barrier = pltpu.get_barrier_semaphore()
    for d in range(1, pairs):
        to = (pair + d) % pairs
        pl.semaphore_signal(barrier, inc=1, device_id=(to * 2 + x, core), device_id_type=MESH)
    pl.semaphore_signal(
        barrier, inc=1, device_id=(pair * 2 + 1 - x, core), device_id_type=MESH
    )
    pl.semaphore_wait(barrier, pairs)

    def kv_copy(c):
        return pltpu.make_async_remote_copy(
            src_ref=proj.at[pl.ds(c * rows, rows), pl.ds(DH, 2 * DH)],
            dst_ref=other.at[pl.ds(c * rows, rows)],
            send_sem=kv_send.at[c], recv_sem=kv_recv.at[c],
            device_id=(pair * 2 + 1 - x, core), device_id_type=MESH,
        )

    for c in range(parts):
        kv_copy(c).start()

    def dot_t(a, b):
        return lax.dot_general(a, b, (((1,), (1,)), ((), ())), preferred_element_type=F32)

    for j in range(pairs):
        here = pl.ds(j * tok, tok)
        count = (j + 1) * tok
        scores = dot_t(proj[here, :DH], proj[:count, DH : 2 * DH]) * scale
        col = lax.broadcasted_iota(jnp.int32, (tok, count), 1)
        row = lax.broadcasted_iota(jnp.int32, (tok, count), 0)
        scores = jnp.where(col <= row + j * tok, scores, -1e30)
        peak = jnp.max(scores, axis=1, keepdims=True)
        expo = jnp.exp(scores - peak)
        top[here] = jnp.broadcast_to(peak, (tok, DH))
        total[here] = jnp.broadcast_to(jnp.sum(expo, axis=1, keepdims=True), (tok, DH))
        accum[here] = jnp.dot(
            expo.astype(BF16), proj[:count, 2 * DH :], preferred_element_type=F32
        )

    def back_copy(j):
        return pltpu.make_async_remote_copy(
            src_ref=result.at[j], dst_ref=out.at[:, pl.ds(pl.multiple_of(pair * DH, DH), DH)],
            send_sem=send.at[j], recv_sem=recv.at[pair],
            device_id=(j * 2 + x, core), device_id_type=MESH,
        )

    for j in range(pairs):
        here = pl.ds(j * tok, tok)
        count = (j + 1) * tok
        if j * tok % rows == 0:
            kv_copy(j * tok // rows).wait_recv()
        scores = dot_t(proj[here, :DH], other[:count, :DH]) * scale
        col = lax.broadcasted_iota(jnp.int32, (tok, count), 1)
        scores = jnp.where(col < (j + x) * tok, scores, -1e30)
        peak = top[here]
        new_peak = jnp.maximum(peak, jnp.max(scores, axis=1, keepdims=True))
        factor = jnp.exp(peak - new_peak)
        expo = jnp.exp(scores - new_peak[:, :1])
        summed = total[here] * factor + jnp.sum(expo, axis=1, keepdims=True)
        value = accum[here] * factor + jnp.dot(
            expo.astype(BF16), other[:count, DH:], preferred_element_type=F32
        )
        result[j] = (value / summed).astype(BF16)

        @pl.when(j != pair)
        def _():
            back_copy(j).start()

    own = pltpu.make_async_copy(
        result.at[pair], out.at[:, pl.ds(pl.multiple_of(pair * DH, DH), DH)], local_sem
    )
    own.start()
    own.wait()
    for c in range(parts):
        kv_copy(c).wait_send()
    for j in range(pairs):

        @pl.when(j != pair)
        def _():
            back_copy(j).wait_send()

    for d in range(1, pairs):
        frm = (pair + d) % pairs
        pltpu.make_async_remote_copy(
            src_ref=result.at[frm],
            dst_ref=out.at[:, pl.ds(pl.multiple_of(frm * DH, DH), DH)],
            send_sem=send.at[frm], recv_sem=recv.at[frm],
            device_id=(frm * 2 + x, core), device_id_type=MESH,
        ).wait_recv()


def attend(projected, pairs, tok):
    vmem = pl.BlockSpec(memory_space=pltpu.VMEM)
    dma = pltpu.SemaphoreType.DMA
    rows = pairs * tok
    parts = 4
    return pl.pallas_call(
        functools.partial(attend_kernel, pairs, tok),
        out_shape=jax.ShapeDtypeStruct((tok, pairs * DH), BF16),
        in_specs=[vmem],
        out_specs=vmem,
        scratch_shapes=[
            pltpu.VMEM((rows, 2 * DH), BF16),
            pltpu.VMEM((rows, DH), F32),
            pltpu.VMEM((rows, DH), F32),
            pltpu.VMEM((rows, DH), F32),
            pltpu.VMEM((pairs, tok, DH), BF16),
            dma,
            dma((parts,)),
            dma((parts,)),
            dma((pairs,)),
            dma((pairs,)),
        ],
        compiler_params=pltpu.CompilerParams(
            collective_id=1, has_side_effects=True, vmem_limit_bytes=32 * 2**20
        ),
    )(projected)


def local_pairs(features, short_taps, long_filter, skip, norm_gain, w_qkv):
    ranks = lax.axis_size("ctx")
    pairs = ranks // 2
    me = lax.axis_index("ctx")
    core = lax.axis_index("tp")
    x = me % 2
    taps = short_taps.shape[0]
    tok = features.shape[2]
    width = features.shape[1] // ranks
    taps_here = lax.dynamic_slice_in_dim(short_taps, me * width, width, 2)
    skip_here = lax.dynamic_slice_in_dim(skip, me * width, width, 0)
    coef = jnp.concatenate([taps_here.reshape(taps * 3, width), skip_here[None]], axis=0).T
    coef = jnp.pad(coef, ((0, 0), (0, DH - coef.shape[1])))
    gathered, w_all = hyena(features, long_filter, w_qkv, coef, ranks // 4, taps)
    channels = norm_gain.shape[0]
    whole = gathered.reshape(channels, pairs * tok)
    half = lax.dynamic_slice(
        gathered,
        (core, 0, 0, 0, (me // 2) * tok),
        (1, pairs, 2, width, tok),
    ).reshape(channels // 2, tok)
    whole_f = whole.astype(F32)
    inverse = lax.rsqrt(jnp.mean(whole_f * whole_f, axis=0, keepdims=True) + 1e-06)
    normed = (whole_f * inverse * norm_gain[:, None]).astype(BF16)
    projected = lax.dot_general(
        normed, w_all.reshape(channels, 3 * DH), (((0,), (0,)), ((), ())),
        preferred_element_type=F32,
    ).astype(BF16)
    attended = attend(projected, pairs, tok)
    return (half, attended)


def solution(mesh):
    in_specs = (
        P(None, "tp", "ctx"),
        P(None, None, "tp"),
        P("tp", "ctx"),
        P("tp"),
        P(),
        P("ctx", None, "tp"),
    )
    out_specs = (P("tp", "ctx"), P("ctx", "tp"))

    def whole(features, short_taps, long_filter, skip, norm_gain, w_qkv):
        heads = w_qkv.shape[2] // mesh.shape["tp"] // DH
        paired = mesh.shape["ctx"] == 16 and heads == 8
        body = local_pairs if paired else local
        return jax.shard_map(
            body, mesh=mesh, in_specs=in_specs, out_specs=out_specs, check_vma=False
        )(features, short_taps, long_filter, skip, norm_gain, w_qkv)

    return whole
```

```python
import functools
import math

import jax
import jax.numpy as jnp
import ml_dtypes
import numpy as np
from jax import lax
from jax.experimental import pallas as pl
from jax.experimental.pallas import tpu as pltpu
from jax.sharding import PartitionSpec as P

DH = 128


HIGHEST = lax.Precision.HIGHEST


def shifted(block, axis, distance):
    devices = range(lax.axis_size(axis))
    route = [(i - distance, i) for i in devices if i - distance in devices]
    return lax.ppermute(block, axis, route)


def angle_table(rows, cols, modulus):
    left = jnp.arange(rows, dtype=jnp.int32)[:, None]
    right = jnp.arange(cols, dtype=jnp.int32)[None, :]
    phase = (left * right % modulus).astype(jnp.float32) * (2.0 * math.pi / modulus)
    return (jnp.cos(phase), jnp.sin(phase))


def contract(form, data, table):
    return jnp.einsum(form, data, table, precision=HIGHEST)


def spectrum(lanes, tok):
    width = lanes.shape[0]
    length = lanes.shape[1]
    outer = 2 * tok
    inner = 2 * length // outer
    data = lanes.reshape(width, tok, inner)
    cos_a, sin_a = angle_table(tok, outer, outer)
    first_re = contract("kaq,ab->kbq", data, cos_a)
    first_im = -contract("kaq,ab->kbq", data, sin_a)
    cos_t, sin_t = angle_table(outer, inner, 2 * length)
    turned_re = first_re * cos_t + first_im * sin_t
    turned_im = first_im * cos_t - first_re * sin_t
    cos_b, sin_b = angle_table(inner, inner, inner)
    out_re = contract("kbq,qr->kbr", turned_re, cos_b) + contract("kbq,qr->kbr", turned_im, sin_b)
    out_im = contract("kbq,qr->kbr", turned_im, cos_b) - contract("kbq,qr->kbr", turned_re, sin_b)
    return (out_re, out_im)


def inverse_real(spec_re, spec_im, tok, length):
    width = spec_re.shape[0]
    outer = 2 * tok
    inner = spec_re.shape[2]
    cos_b, sin_b = angle_table(inner, inner, inner)
    back_re = contract("kbr,rq->kbq", spec_re, cos_b) - contract("kbr,rq->kbq", spec_im, sin_b)
    back_im = contract("kbr,rq->kbq", spec_im, cos_b) + contract("kbr,rq->kbq", spec_re, sin_b)
    cos_t, sin_t = angle_table(outer, inner, 2 * length)
    turned_re = back_re * cos_t - back_im * sin_t
    turned_im = back_im * cos_t + back_re * sin_t
    cos_a, sin_a = angle_table(outer, tok, outer)
    real = contract("kbq,ba->kaq", turned_re, cos_a) - contract("kbq,ba->kaq", turned_im, sin_a)
    return (real / (2 * length)).reshape(width, length)


def attend_rows(query_rows, query_pos, keyvals, count, block):
    rows = query_rows.shape[0]
    scale = DH ** (-0.5)
    start_state = (
        jnp.full((rows,), -1e30, jnp.float32),
        jnp.zeros((rows,), jnp.float32),
        jnp.zeros((rows, DH), jnp.float32),
    )

    def step(index, state):
        running, total, accum = state
        part = lax.dynamic_slice_in_dim(keyvals, index * block, block, 0)
        keys = part[:, :DH]
        vals = part[:, DH:]
        scores = (
            lax.dot_general(
                query_rows, keys, (((1,), (1,)), ((), ())), preferred_element_type=jnp.float32
            )
            * scale
        )
        key_pos = index * block + jnp.arange(block, dtype=jnp.int32)
        allowed = key_pos[None, :] <= query_pos[:, None]
        scores = jnp.where(allowed, scores, -1e30)
        new_top = jnp.maximum(running, jnp.max(scores, axis=1))
        factor = jnp.exp(running - new_top)
        expo = jnp.where(allowed, jnp.exp(scores - new_top[:, None]), 0.0)
        total = total * factor + jnp.sum(expo, axis=1)
        accum = accum * factor[:, None] + jnp.dot(
            expo.astype(jnp.bfloat16), vals, preferred_element_type=jnp.float32
        )
        return (new_top, total, accum)

    running, total, accum = lax.fori_loop(0, count, step, start_state)
    return accum / total[:, None]


def local(features, short_taps, long_filter, skip, norm_gain, w_qkv):
    taps = short_taps.shape[0]
    tok = features.shape[2]
    rim = shifted(features[:, :, tok - (taps - 1) :], "ctx", 1)
    extended = jnp.concatenate([rim, features], axis=2).astype(jnp.float32)
    short = short_taps[0][:, :, None] * extended[:, :, taps - 1 : taps - 1 + tok]
    for lag in range(1, taps):
        short = (
            short
            + short_taps[lag][:, :, None] * extended[:, :, taps - 1 - lag : taps - 1 - lag + tok]
        )
    carried = (short[1] * short[2]).astype(jnp.bfloat16)
    lanes = lax.all_to_all(carried, "ctx", split_axis=0, concat_axis=1, tiled=True).astype(
        jnp.float32
    )
    filt = lax.all_to_all(long_filter, "ctx", split_axis=0, concat_axis=1, tiled=True)
    length = lanes.shape[1]
    data_re, data_im = spectrum(lanes, tok)
    filt_re, filt_im = spectrum(filt, tok)
    conv = inverse_real(
        data_re * filt_re - data_im * filt_im, data_re * filt_im + data_im * filt_re, tok, length
    )
    long_back = lax.all_to_all(
        conv.astype(jnp.bfloat16), "ctx", split_axis=1, concat_axis=0, tiled=True
    )
    mixed = (
        short[0] * (long_back.astype(jnp.float32) + skip[:, None] * carried.astype(jnp.float32))
    ).astype(jnp.bfloat16)
    whole = lax.all_gather(mixed, "tp", axis=0, tiled=True)
    whole_f = whole.astype(jnp.float32)
    inverse = lax.rsqrt(jnp.mean(whole_f * whole_f, axis=0, keepdims=True) + 1e-06)
    normed = (whole_f * inverse * norm_gain[:, None]).astype(jnp.bfloat16)
    columns = w_qkv.shape[1] * w_qkv.shape[2]
    piece = lax.all_gather(w_qkv, "ctx", axis=0, tiled=True)
    count = piece.shape[0]
    projected = lax.dot_general(
        normed,
        piece.reshape(count, columns),
        (((0,), (0,)), ((), ())),
        preferred_element_type=jnp.float32,
    )
    heads = w_qkv.shape[2] // DH
    projected = projected.astype(jnp.bfloat16).reshape(tok, 3, heads, DH)
    ranks = lax.axis_size("ctx")
    subs = ranks // heads
    sub = tok // subs
    key_pairs = jnp.concatenate([projected[:, 1], projected[:, 2]], axis=-1)
    slot = lax.axis_index("ctx") % subs
    queries = jnp.transpose(projected[:, 0].reshape(subs, sub, heads, DH), (2, 0, 1, 3)).reshape(
        ranks, sub, DH
    )
    pairs = jnp.transpose(key_pairs, (1, 0, 2))
    pairs = jnp.broadcast_to(pairs[:, None], (heads, subs, tok, 2 * DH)).reshape(ranks, tok, 2 * DH)
    got_queries = lax.all_to_all(queries, "ctx", split_axis=0, concat_axis=0, tiled=True).reshape(
        ranks * sub, DH
    )
    got_pairs = lax.all_to_all(pairs, "ctx", split_axis=0, concat_axis=0, tiled=True).reshape(
        ranks * tok, 2 * DH
    )
    source = jnp.arange(ranks * sub, dtype=jnp.int32)
    query_pos = source // sub * tok + slot * sub + source % sub
    total_keys = ranks * tok
    block = min(2048, total_keys)
    result = attend_rows(got_queries, query_pos, got_pairs, total_keys // block, block)
    result = result.astype(jnp.bfloat16).reshape(ranks, sub, DH)
    back = lax.all_to_all(result, "ctx", split_axis=0, concat_axis=0, tiled=True)
    attended = jnp.transpose(back.reshape(heads, subs, sub, DH), (1, 2, 0, 3)).reshape(
        tok, heads * DH
    )
    return (mixed, attended)


MESH = pl.DeviceIdType.MESH
F32 = jnp.float32
BF16 = jnp.bfloat16


def split_table(table):
    high = table.astype(ml_dtypes.bfloat16)
    low = (table - high.astype(np.float64)).astype(ml_dtypes.bfloat16)
    return [high, low]


def packed_tables(tok):
    full = 2 * tok
    pos = np.arange(tok)[:, None]
    freq = np.arange(tok)[None, :]
    angle = 2.0 * np.pi * ((pos * freq) % full) / full
    imag = -np.sin(angle)
    imag[:, 0] = (-1.0) ** np.arange(tok)
    forward = np.concatenate([np.cos(angle), imag], axis=1)
    out = np.arange(full)[None, :]
    freq = np.arange(tok)[:, None]
    angle = 2.0 * np.pi * ((out * freq) % full) / full
    real = 2.0 * np.cos(angle)
    real[0] = 1.0
    imag = -2.0 * np.sin(angle)
    imag[0] = (-1.0) ** np.arange(full)
    backward = np.concatenate([real, imag], axis=0) / full
    return np.concatenate(split_table(forward) + split_table(backward), axis=0)


def hyena_kernel(
    dims,
    feats,
    filt_in,
    w_in,
    coef_in,
    tables_in,
    gathered,
    w_all,
    filt_wide,
    filt,
    w_raw,
    wts,
    coef,
    wide_coef,
    spec_hi,
    spec_lo,
    waves,
    tables,
    feat_all,
    filt_all,
    short0,
    carried,
    spec_x,
    spec_f,
    mixed,
    local_sem,
    feat_send,
    feat_recv,
    filt_send,
    filt_recv,
    w_send,
    w_recv,
    wx_send,
    wx_recv,
    x_send,
    x_recv,
    z_send,
    z_recv,
    y_send,
    y_recv,
    s_send,
    s_recv,
):
    ranks, nz, taps = dims
    me = lax.axis_index("ctx")
    core = lax.axis_index("tp")
    x = me % 2
    pair = me // 2
    y = pair % 2
    z = pair // 2
    width = filt_all.shape[1]
    tok = filt_all.shape[2]
    pairs = ranks // 2

    barrier = pltpu.get_barrier_semaphore()

    def greet(d, _):
        pl.semaphore_signal(
            barrier, inc=1, device_id=((me + d) % ranks, core), device_id_type=MESH
        )
        return 0

    lax.fori_loop(1, ranks, greet, 0)
    pl.semaphore_signal(barrier, inc=1, device_id=(me, 1 - core), device_id_type=MESH)
    pl.semaphore_wait(barrier, ranks)

    def remote(src, dst, send, recv, ctx, tp):
        return pltpu.make_async_remote_copy(
            src_ref=src, dst_ref=dst, send_sem=send, recv_sem=recv,
            device_id=(ctx, tp), device_id_type=MESH,
        )

    def feat_copy(d):
        to = (me + d) % ranks
        return remote(
            feats.at[:, pl.ds(to * width, width)], feat_all.at[me],
            feat_send.at[d], feat_recv.at[d], to, core,
        )

    def filt_copy(d):
        to = (me + d) % ranks
        return remote(
            filt.at[pl.ds(to * width, width)], filt_all.at[me],
            filt_send.at[d], filt_recv.at[d], to, core,
        )

    def w_copy(d):
        to = (pair + d) % pairs
        return remote(
            wts.at[to], w_all.at[pair, x], w_send.at[d], w_recv.at[d], to * 2 + x, core
        )

    loads = [
        pltpu.make_async_copy(src, dst, local_sem.at[4 + i])
        for i, (src, dst) in enumerate(
            (
                (filt_in, filt_wide),
                (w_in, w_raw),
                (coef_in, coef),
                (tables_in, tables),
            )
        )
    ]
    for d in range(1, ranks):
        feat_copy(d).start()
    for load in loads:
        load.start()
    own = [
        pltpu.make_async_copy(
            feats.at[:, pl.ds(me * width, width)], feat_all.at[me], local_sem.at[0]
        ),
        pltpu.make_async_copy(filt.at[pl.ds(me * width, width)], filt_all.at[me], local_sem.at[1]),
        pltpu.make_async_copy(wts.at[pair], w_all.at[pair, x], local_sem.at[2]),
    ]
    own[0].start()
    loads[0].wait()
    filt[...] = filt_wide[...].astype(BF16)
    own[1].start()
    for d in range(1, ranks):
        filt_copy(d).start()
    loads[1].wait()
    for i in range(3):
        for h in range(pairs):
            wts[h, :, i * DH : (i + 1) * DH] = w_raw[:, i, h * DH : (h + 1) * DH]
    own[2].start()
    for load in loads[2:]:
        load.wait()
    for i in range(3 * taps + 1):
        wide_coef[i] = jnp.broadcast_to(coef[:, i : i + 1], (width, tok))
    own[0].wait()
    own[1].wait()
    for d in range(1, ranks):
        feat_copy(d).wait_recv()
    for d in range(1, pairs):
        w_copy(d).start()

    lane = lax.broadcasted_iota(jnp.int32, (width, tok), 1)

    def short_block(b, _):
        before = jnp.maximum(b - 1, 0)
        live = jnp.where(b > 0, 1.0, 0.0).astype(F32)
        sums = []
        for i in range(3):
            now = feat_all[b, i].astype(F32)
            past = feat_all[before, i].astype(F32) * live
            total = wide_coef[i] * now
            for lag in range(1, taps):
                moved = pltpu.roll(jnp.where(lane < tok - lag, now, past), lag, 1)
                total = total + wide_coef[lag * 3 + i] * moved
            sums.append(total)
        short0[b] = sums[0]
        carried[b] = (sums[1] * sums[2]).astype(BF16)
        return 0

    lax.fori_loop(0, ranks, short_block, 0)

    group = 4
    fwd_hi = tables.at[pl.ds(0, tok)]
    fwd_lo = tables.at[pl.ds(tok, tok)]
    inv_hi = tables.at[pl.ds(2 * tok, 2 * tok)]
    inv_lo = tables.at[pl.ds(4 * tok, 2 * tok)]

    def spectra(blocks):
        rows = blocks.reshape(group * width, tok)
        spec = jnp.dot(rows, fwd_hi[...], preferred_element_type=F32) + jnp.dot(
            rows, fwd_lo[...], preferred_element_type=F32
        )
        return spec.reshape(group, width, 2 * tok)

    def data_group(g, _):
        here = pl.ds(g * group, group)
        spec_x[here] = spectra(carried[here])
        return 0

    lax.fori_loop(0, ranks // group, data_group, 0)
    for d in range(1, ranks):
        filt_copy(d).wait_recv()

    def filter_group(g, _):
        here = pl.ds(g * group, group)
        spec = spectra(filt_all[here])
        real = spec[:, :, :tok]
        imag = spec[:, :, tok:]
        zero = lax.broadcasted_iota(jnp.int32, imag.shape, 2) == 0
        spec_f[here, 0] = real
        spec_f[here, 1] = jnp.where(zero, 0.0, imag)
        spec_f[here, 2] = jnp.where(zero, imag, real)
        return 0

    lax.fori_loop(0, ranks // group, filter_group, 0)

    def block(m, _):
        def term(d, acc):
            real, imag = acc
            xr = spec_x[m - d, :, :tok]
            xi = spec_x[m - d, :, tok:]
            f_re = spec_f[d, 0]
            f_im = spec_f[d, 1]
            f_ny = spec_f[d, 2]
            return (real + (xr * f_re - xi * f_im), imag + (xr * f_im + xi * f_ny))

        zero = jnp.zeros((width, tok), F32)
        real, imag = lax.fori_loop(0, m + 1, term, (zero, zero))
        rows = pl.ds(pl.multiple_of(m * width, width), width)
        for at, part in enumerate((real, imag)):
            high = part.astype(BF16)
            spec_hi[rows, at * tok : (at + 1) * tok] = high
            spec_lo[rows, at * tok : (at + 1) * tok] = (part - high.astype(F32)).astype(BF16)
        return 0

    lax.fori_loop(0, ranks, block, 0)

    def inverse_group(g, _):
        rows = pl.ds(pl.multiple_of(g * group * width, group * width), group * width)
        high = spec_hi[rows]
        wave = (
            jnp.dot(high, inv_hi[...], preferred_element_type=F32)
            + jnp.dot(spec_lo[rows], inv_hi[...], preferred_element_type=F32)
            + jnp.dot(high, inv_lo[...], preferred_element_type=F32)
        )
        waves[pl.ds(g * group, group)] = wave.reshape(group, width, 2 * tok)
        return 0

    lax.fori_loop(0, ranks // group, inverse_group, 0)

    def finish(m, _):
        live = jnp.where(m > 0, 1.0, 0.0).astype(F32)
        tail = waves[jnp.maximum(m - 1, 0), :, tok:] * live
        long_out = (waves[m, :, :tok] + tail).astype(BF16).astype(F32)
        value = short0[m] * (long_out + wide_coef[3 * taps] * carried[m].astype(F32))
        mixed[m % 2, :, pl.ds(pl.multiple_of((m // 2) * tok, tok), tok)] = value.astype(BF16)
        return 0

    lax.fori_loop(0, ranks, finish, 0)

    keep = pltpu.make_async_copy(mixed.at[x], gathered.at[core, pair, x], local_sem.at[3])
    keep.start()
    swap = remote(
        mixed.at[1 - x], gathered.at[core, pair, x], x_send.at[0], x_recv.at[0],
        pair * 2 + 1 - x, core,
    )
    swap.start()
    keep.wait()
    swap.wait_recv()

    def chunk(p):
        return gathered.at[core, p]

    def up_copy(hop):
        p = (z - hop) * 2 + y
        return remote(
            chunk(p), chunk(p), z_send.at[hop], z_recv.at[hop + 1],
            (z + 1) * 4 + y * 2 + x, core,
        )

    def down_copy(hop):
        p = (z + hop) * 2 + y
        return remote(
            chunk(p), chunk(p), z_send.at[nz + hop], z_recv.at[nz + hop + 1],
            (z - 1) * 4 + y * 2 + x, core,
        )

    def y_copy(origin):
        p = origin * 2 + y
        return remote(
            chunk(p), chunk(p), y_send.at[origin], y_recv.at[origin],
            z * 4 + (1 - y) * 2 + x, core,
        )

    def s_copy(origin, side):
        p = origin * 2 + jnp.where(side == 0, y, 1 - y)
        return remote(
            chunk(p), chunk(p), s_send.at[side * nz + origin], s_recv.at[side * nz + origin],
            me, 1 - core,
        )

    def arrived(hop, up):
        p = (z - hop if up else z + hop) * 2 + y
        at = hop if up else nz + hop
        remote(
            chunk(p), chunk(p), z_send.at[0], z_recv.at[at],
            (z - 1 if up else z + 1) * 4 + y * 2 + x, core,
        ).wait_recv()

    @pl.when(z < nz - 1)
    def _():
        up_copy(0).start()

    @pl.when(z > 0)
    def _():
        down_copy(0).start()

    y_copy(z).start()
    s_copy(z, 0).start()

    own[2].wait()
    for d in range(1, pairs):
        w_copy(d).wait_recv()
    w_swap = remote(
        w_all.at[:, x], w_all.at[:, x], wx_send.at[0], wx_recv.at[0], pair * 2 + 1 - x, core
    )
    w_swap.start()

    for hop in range(1, nz):

        @pl.when(z - hop >= 0)
        def _():
            arrived(hop, True)

            @pl.when(z < nz - 1)
            def _():
                up_copy(hop).start()

            y_copy(z - hop).start()
            s_copy(z - hop, 0).start()

        @pl.when(z + hop < nz)
        def _():
            arrived(hop, False)

            @pl.when(z > 0)
            def _():
                down_copy(hop).start()

            y_copy(z + hop).start()
            s_copy(z + hop, 0).start()

    for hop in range(nz):

        @pl.when(z - hop >= 0)
        def _():
            y_copy(z - hop).wait_recv()
            s_copy(z - hop, 1).start()

        if hop > 0:

            @pl.when(z + hop < nz)
            def _():
                y_copy(z + hop).wait_recv()
                s_copy(z + hop, 1).start()

    for origin in range(nz):
        s_copy(origin, 0).wait_recv()
        s_copy(origin, 1).wait_recv()
    w_swap.wait()
    for d in range(1, ranks):
        feat_copy(d).wait_send()
        filt_copy(d).wait_send()
    for d in range(1, pairs):
        w_copy(d).wait_send()
    swap.wait_send()
    for hop in range(nz):

        @pl.when((z < nz - 1) & (z - hop >= 0))
        def _():
            up_copy(hop).wait_send()

        @pl.when((z > 0) & (z + hop < nz))
        def _():
            down_copy(hop).wait_send()

    for origin in range(nz):
        y_copy(origin).wait_send()
        s_copy(origin, 0).wait_send()
        s_copy(origin, 1).wait_send()


def hyena(features, filt, w_qkv, coef, nz, taps):
    ranks = features.shape[1] // coef.shape[0]
    width = coef.shape[0]
    tok = features.shape[2]
    pairs = ranks // 2
    rows = w_qkv.shape[0]
    columns = 3 * DH
    tables = jnp.asarray(packed_tables(tok))
    hbm = pl.BlockSpec(memory_space=pl.ANY)
    dma = pltpu.SemaphoreType.DMA
    return pl.pallas_call(
        functools.partial(hyena_kernel, (ranks, nz, taps)),
        out_shape=(
            jax.ShapeDtypeStruct((2, pairs, 2, width, pairs * tok), BF16),
            jax.ShapeDtypeStruct((pairs, 2, rows, columns), BF16),
        ),
        in_specs=[hbm] * 5,
        out_specs=(hbm, hbm),
        scratch_shapes=[
            pltpu.VMEM(filt.shape, F32),
            pltpu.VMEM(filt.shape, BF16),
            pltpu.VMEM(w_qkv.shape, BF16),
            pltpu.VMEM((pairs, rows, columns), BF16),
            pltpu.VMEM(coef.shape, F32),
            pltpu.VMEM((3 * taps + 1, width, tok), F32),
            pltpu.VMEM((ranks * width, 2 * tok), BF16),
            pltpu.VMEM((ranks * width, 2 * tok), BF16),
            pltpu.VMEM((ranks, width, 2 * tok), F32),
        ]
        + [pltpu.VMEM(tables.shape, BF16)]
        + [
            pltpu.VMEM((ranks, 3, width, tok), BF16),
            pltpu.VMEM((ranks, width, tok), BF16),
            pltpu.VMEM((ranks, width, tok), F32),
            pltpu.VMEM((ranks, width, tok), BF16),
            pltpu.VMEM((ranks, width, 2 * tok), F32),
            pltpu.VMEM((ranks, 3, width, tok), F32),
            pltpu.VMEM((2, width, pairs * tok), BF16),
            dma((8,)),
            dma((ranks,)),
            dma((ranks,)),
            dma((ranks,)),
            dma((ranks,)),
            dma((pairs,)),
            dma((pairs,)),
            dma((1,)),
            dma((1,)),
            dma((1,)),
            dma((1,)),
            dma((2 * nz,)),
            dma((2 * nz,)),
            dma((nz,)),
            dma((nz,)),
            dma((2 * nz,)),
            dma((2 * nz,)),
        ],
        compiler_params=pltpu.CompilerParams(
            collective_id=0, has_side_effects=True, vmem_limit_bytes=60 * 2**20
        ),
    )(features, filt, w_qkv, coef, tables)


def attend_kernel(
    pairs, tok, proj, out, other, top, total, accum, result,
    local_sem, kv_send, kv_recv, send, recv,
):
    me = lax.axis_index("ctx")
    core = lax.axis_index("tp")
    x = me % 2
    pair = me // 2
    parts = kv_send.shape[0]
    rows = pairs * tok // parts
    scale = DH ** (-0.5)

    barrier = pltpu.get_barrier_semaphore()
    for d in range(1, pairs):
        to = (pair + d) % pairs
        pl.semaphore_signal(barrier, inc=1, device_id=(to * 2 + x, core), device_id_type=MESH)
    pl.semaphore_signal(
        barrier, inc=1, device_id=(pair * 2 + 1 - x, core), device_id_type=MESH
    )
    pl.semaphore_wait(barrier, pairs)

    def kv_copy(c):
        return pltpu.make_async_remote_copy(
            src_ref=proj.at[pl.ds(c * rows, rows), pl.ds(DH, 2 * DH)],
            dst_ref=other.at[pl.ds(c * rows, rows)],
            send_sem=kv_send.at[c], recv_sem=kv_recv.at[c],
            device_id=(pair * 2 + 1 - x, core), device_id_type=MESH,
        )

    for c in range(parts):
        kv_copy(c).start()

    def dot_t(a, b):
        return lax.dot_general(a, b, (((1,), (1,)), ((), ())), preferred_element_type=F32)

    for j in range(pairs):
        here = pl.ds(j * tok, tok)
        count = (j + 1) * tok
        scores = dot_t(proj[here, :DH], proj[:count, DH : 2 * DH]) * scale
        col = lax.broadcasted_iota(jnp.int32, (tok, count), 1)
        row = lax.broadcasted_iota(jnp.int32, (tok, count), 0)
        scores = jnp.where(col <= row + j * tok, scores, -1e30)
        peak = jnp.max(scores, axis=1, keepdims=True)
        expo = jnp.exp(scores - peak)
        top[here] = jnp.broadcast_to(peak, (tok, DH))
        total[here] = jnp.broadcast_to(jnp.sum(expo, axis=1, keepdims=True), (tok, DH))
        accum[here] = jnp.dot(
            expo.astype(BF16), proj[:count, 2 * DH :], preferred_element_type=F32
        )

    def back_copy(j):
        return pltpu.make_async_remote_copy(
            src_ref=result.at[j], dst_ref=out.at[:, pl.ds(pl.multiple_of(pair * DH, DH), DH)],
            send_sem=send.at[j], recv_sem=recv.at[pair],
            device_id=(j * 2 + x, core), device_id_type=MESH,
        )

    for j in range(pairs):
        here = pl.ds(j * tok, tok)
        count = (j + 1) * tok
        if j * tok % rows == 0:
            kv_copy(j * tok // rows).wait_recv()
        scores = dot_t(proj[here, :DH], other[:count, :DH]) * scale
        col = lax.broadcasted_iota(jnp.int32, (tok, count), 1)
        scores = jnp.where(col < (j + x) * tok, scores, -1e30)
        peak = top[here]
        new_peak = jnp.maximum(peak, jnp.max(scores, axis=1, keepdims=True))
        factor = jnp.exp(peak - new_peak)
        expo = jnp.exp(scores - new_peak[:, :1])
        summed = total[here] * factor + jnp.sum(expo, axis=1, keepdims=True)
        value = accum[here] * factor + jnp.dot(
            expo.astype(BF16), other[:count, DH:], preferred_element_type=F32
        )
        result[j] = (value / summed).astype(BF16)

        @pl.when(j != pair)
        def _():
            back_copy(j).start()

    own = pltpu.make_async_copy(
        result.at[pair], out.at[:, pl.ds(pl.multiple_of(pair * DH, DH), DH)], local_sem
    )
    own.start()
    own.wait()
    for c in range(parts):
        kv_copy(c).wait_send()
    for j in range(pairs):

        @pl.when(j != pair)
        def _():
            back_copy(j).wait_send()

    for d in range(1, pairs):
        frm = (pair + d) % pairs
        pltpu.make_async_remote_copy(
            src_ref=result.at[frm],
            dst_ref=out.at[:, pl.ds(pl.multiple_of(frm * DH, DH), DH)],
            send_sem=send.at[frm], recv_sem=recv.at[frm],
            device_id=(frm * 2 + x, core), device_id_type=MESH,
        ).wait_recv()


def attend(projected, pairs, tok):
    vmem = pl.BlockSpec(memory_space=pltpu.VMEM)
    dma = pltpu.SemaphoreType.DMA
    rows = pairs * tok
    parts = 4
    return pl.pallas_call(
        functools.partial(attend_kernel, pairs, tok),
        out_shape=jax.ShapeDtypeStruct((tok, pairs * DH), BF16),
        in_specs=[vmem],
        out_specs=vmem,
        scratch_shapes=[
            pltpu.VMEM((rows, 2 * DH), BF16),
            pltpu.VMEM((rows, DH), F32),
            pltpu.VMEM((rows, DH), F32),
            pltpu.VMEM((rows, DH), F32),
            pltpu.VMEM((pairs, tok, DH), BF16),
            dma,
            dma((parts,)),
            dma((parts,)),
            dma((pairs,)),
            dma((pairs,)),
        ],
        compiler_params=pltpu.CompilerParams(
            collective_id=1, has_side_effects=True, vmem_limit_bytes=32 * 2**20
        ),
    )(projected)


def local_pairs(features, short_taps, long_filter, skip, norm_gain, w_qkv):
    ranks = lax.axis_size("ctx")
    pairs = ranks // 2
    me = lax.axis_index("ctx")
    core = lax.axis_index("tp")
    x = me % 2
    taps = short_taps.shape[0]
    tok = features.shape[2]
    width = features.shape[1] // ranks
    taps_here = lax.dynamic_slice_in_dim(short_taps, me * width, width, 2)
    skip_here = lax.dynamic_slice_in_dim(skip, me * width, width, 0)
    coef = jnp.concatenate([taps_here.reshape(taps * 3, width), skip_here[None]], axis=0).T
    coef = jnp.pad(coef, ((0, 0), (0, DH - coef.shape[1])))
    gathered, w_all = hyena(features, long_filter, w_qkv, coef, ranks // 4, taps)
    channels = norm_gain.shape[0]
    whole = gathered.reshape(channels, pairs * tok)
    half = lax.dynamic_slice(
        gathered,
        (core, 0, 0, 0, (me // 2) * tok),
        (1, pairs, 2, width, tok),
    ).reshape(channels // 2, tok)
    whole_f = whole.astype(F32)
    inverse = lax.rsqrt(jnp.mean(whole_f * whole_f, axis=0, keepdims=True) + 1e-06)
    normed = (whole_f * inverse * norm_gain[:, None]).astype(BF16)
    projected = lax.dot_general(
        normed, w_all.reshape(channels, 3 * DH), (((0,), (0,)), ((), ())),
        preferred_element_type=F32,
    ).astype(BF16)
    attended = attend(projected, pairs, tok)
    return (half, attended)


def solution(mesh):
    in_specs = (
        P(None, "tp", "ctx"),
        P(None, None, "tp"),
        P("tp", "ctx"),
        P("tp"),
        P(),
        P("ctx", None, "tp"),
    )
    out_specs = (P("tp", "ctx"), P("ctx", "tp"))

    def whole(features, short_taps, long_filter, skip, norm_gain, w_qkv):
        heads = w_qkv.shape[2] // mesh.shape["tp"] // DH
        paired = mesh.shape["ctx"] == 16 and heads == 8
        body = local_pairs if paired else local
        return jax.shard_map(
            body, mesh=mesh, in_specs=in_specs, out_specs=out_specs, check_vma=False
        )(features, short_taps, long_filter, skip, norm_gain, w_qkv)

    return whole
```

```python
import functools
import math

import jax
import jax.numpy as jnp
import ml_dtypes
import numpy as np
from jax import lax
from jax.experimental import pallas as pl
from jax.experimental.pallas import tpu as pltpu
from jax.sharding import PartitionSpec as P

DH = 128


HIGHEST = lax.Precision.HIGHEST


def shifted(block, axis, distance):
    devices = range(lax.axis_size(axis))
    route = [(i - distance, i) for i in devices if i - distance in devices]
    return lax.ppermute(block, axis, route)


def angle_table(rows, cols, modulus):
    left = jnp.arange(rows, dtype=jnp.int32)[:, None]
    right = jnp.arange(cols, dtype=jnp.int32)[None, :]
    phase = (left * right % modulus).astype(jnp.float32) * (2.0 * math.pi / modulus)
    return (jnp.cos(phase), jnp.sin(phase))


def contract(form, data, table):
    return jnp.einsum(form, data, table, precision=HIGHEST)


def spectrum(lanes, tok):
    width = lanes.shape[0]
    length = lanes.shape[1]
    outer = 2 * tok
    inner = 2 * length // outer
    data = lanes.reshape(width, tok, inner)
    cos_a, sin_a = angle_table(tok, outer, outer)
    first_re = contract("kaq,ab->kbq", data, cos_a)
    first_im = -contract("kaq,ab->kbq", data, sin_a)
    cos_t, sin_t = angle_table(outer, inner, 2 * length)
    turned_re = first_re * cos_t + first_im * sin_t
    turned_im = first_im * cos_t - first_re * sin_t
    cos_b, sin_b = angle_table(inner, inner, inner)
    out_re = contract("kbq,qr->kbr", turned_re, cos_b) + contract("kbq,qr->kbr", turned_im, sin_b)
    out_im = contract("kbq,qr->kbr", turned_im, cos_b) - contract("kbq,qr->kbr", turned_re, sin_b)
    return (out_re, out_im)


def inverse_real(spec_re, spec_im, tok, length):
    width = spec_re.shape[0]
    outer = 2 * tok
    inner = spec_re.shape[2]
    cos_b, sin_b = angle_table(inner, inner, inner)
    back_re = contract("kbr,rq->kbq", spec_re, cos_b) - contract("kbr,rq->kbq", spec_im, sin_b)
    back_im = contract("kbr,rq->kbq", spec_im, cos_b) + contract("kbr,rq->kbq", spec_re, sin_b)
    cos_t, sin_t = angle_table(outer, inner, 2 * length)
    turned_re = back_re * cos_t - back_im * sin_t
    turned_im = back_im * cos_t + back_re * sin_t
    cos_a, sin_a = angle_table(outer, tok, outer)
    real = contract("kbq,ba->kaq", turned_re, cos_a) - contract("kbq,ba->kaq", turned_im, sin_a)
    return (real / (2 * length)).reshape(width, length)


def attend_rows(query_rows, query_pos, keyvals, count, block):
    rows = query_rows.shape[0]
    scale = DH ** (-0.5)
    start_state = (
        jnp.full((rows,), -1e30, jnp.float32),
        jnp.zeros((rows,), jnp.float32),
        jnp.zeros((rows, DH), jnp.float32),
    )

    def step(index, state):
        running, total, accum = state
        part = lax.dynamic_slice_in_dim(keyvals, index * block, block, 0)
        keys = part[:, :DH]
        vals = part[:, DH:]
        scores = (
            lax.dot_general(
                query_rows, keys, (((1,), (1,)), ((), ())), preferred_element_type=jnp.float32
            )
            * scale
        )
        key_pos = index * block + jnp.arange(block, dtype=jnp.int32)
        allowed = key_pos[None, :] <= query_pos[:, None]
        scores = jnp.where(allowed, scores, -1e30)
        new_top = jnp.maximum(running, jnp.max(scores, axis=1))
        factor = jnp.exp(running - new_top)
        expo = jnp.where(allowed, jnp.exp(scores - new_top[:, None]), 0.0)
        total = total * factor + jnp.sum(expo, axis=1)
        accum = accum * factor[:, None] + jnp.dot(
            expo.astype(jnp.bfloat16), vals, preferred_element_type=jnp.float32
        )
        return (new_top, total, accum)

    running, total, accum = lax.fori_loop(0, count, step, start_state)
    return accum / total[:, None]


def local(features, short_taps, long_filter, skip, norm_gain, w_qkv):
    taps = short_taps.shape[0]
    tok = features.shape[2]
    rim = shifted(features[:, :, tok - (taps - 1) :], "ctx", 1)
    extended = jnp.concatenate([rim, features], axis=2).astype(jnp.float32)
    short = short_taps[0][:, :, None] * extended[:, :, taps - 1 : taps - 1 + tok]
    for lag in range(1, taps):
        short = (
            short
            + short_taps[lag][:, :, None] * extended[:, :, taps - 1 - lag : taps - 1 - lag + tok]
        )
    carried = (short[1] * short[2]).astype(jnp.bfloat16)
    lanes = lax.all_to_all(carried, "ctx", split_axis=0, concat_axis=1, tiled=True).astype(
        jnp.float32
    )
    filt = lax.all_to_all(long_filter, "ctx", split_axis=0, concat_axis=1, tiled=True)
    length = lanes.shape[1]
    data_re, data_im = spectrum(lanes, tok)
    filt_re, filt_im = spectrum(filt, tok)
    conv = inverse_real(
        data_re * filt_re - data_im * filt_im, data_re * filt_im + data_im * filt_re, tok, length
    )
    long_back = lax.all_to_all(
        conv.astype(jnp.bfloat16), "ctx", split_axis=1, concat_axis=0, tiled=True
    )
    mixed = (
        short[0] * (long_back.astype(jnp.float32) + skip[:, None] * carried.astype(jnp.float32))
    ).astype(jnp.bfloat16)
    whole = lax.all_gather(mixed, "tp", axis=0, tiled=True)
    whole_f = whole.astype(jnp.float32)
    inverse = lax.rsqrt(jnp.mean(whole_f * whole_f, axis=0, keepdims=True) + 1e-06)
    normed = (whole_f * inverse * norm_gain[:, None]).astype(jnp.bfloat16)
    columns = w_qkv.shape[1] * w_qkv.shape[2]
    piece = lax.all_gather(w_qkv, "ctx", axis=0, tiled=True)
    count = piece.shape[0]
    projected = lax.dot_general(
        normed,
        piece.reshape(count, columns),
        (((0,), (0,)), ((), ())),
        preferred_element_type=jnp.float32,
    )
    heads = w_qkv.shape[2] // DH
    projected = projected.astype(jnp.bfloat16).reshape(tok, 3, heads, DH)
    ranks = lax.axis_size("ctx")
    subs = ranks // heads
    sub = tok // subs
    key_pairs = jnp.concatenate([projected[:, 1], projected[:, 2]], axis=-1)
    slot = lax.axis_index("ctx") % subs
    queries = jnp.transpose(projected[:, 0].reshape(subs, sub, heads, DH), (2, 0, 1, 3)).reshape(
        ranks, sub, DH
    )
    pairs = jnp.transpose(key_pairs, (1, 0, 2))
    pairs = jnp.broadcast_to(pairs[:, None], (heads, subs, tok, 2 * DH)).reshape(ranks, tok, 2 * DH)
    got_queries = lax.all_to_all(queries, "ctx", split_axis=0, concat_axis=0, tiled=True).reshape(
        ranks * sub, DH
    )
    got_pairs = lax.all_to_all(pairs, "ctx", split_axis=0, concat_axis=0, tiled=True).reshape(
        ranks * tok, 2 * DH
    )
    source = jnp.arange(ranks * sub, dtype=jnp.int32)
    query_pos = source // sub * tok + slot * sub + source % sub
    total_keys = ranks * tok
    block = min(2048, total_keys)
    result = attend_rows(got_queries, query_pos, got_pairs, total_keys // block, block)
    result = result.astype(jnp.bfloat16).reshape(ranks, sub, DH)
    back = lax.all_to_all(result, "ctx", split_axis=0, concat_axis=0, tiled=True)
    attended = jnp.transpose(back.reshape(heads, subs, sub, DH), (1, 2, 0, 3)).reshape(
        tok, heads * DH
    )
    return (mixed, attended)


MESH = pl.DeviceIdType.MESH
F32 = jnp.float32
BF16 = jnp.bfloat16


def split_table(table):
    high = table.astype(ml_dtypes.bfloat16)
    low = (table - high.astype(np.float64)).astype(ml_dtypes.bfloat16)
    return [high, low]


def packed_tables(tok):
    full = 2 * tok
    pos = np.arange(tok)[:, None]
    freq = np.arange(tok)[None, :]
    angle = 2.0 * np.pi * ((pos * freq) % full) / full
    imag = -np.sin(angle)
    imag[:, 0] = (-1.0) ** np.arange(tok)
    forward = np.concatenate([np.cos(angle), imag], axis=1)
    out = np.arange(full)[None, :]
    freq = np.arange(tok)[:, None]
    angle = 2.0 * np.pi * ((out * freq) % full) / full
    real = 2.0 * np.cos(angle)
    real[0] = 1.0
    imag = -2.0 * np.sin(angle)
    imag[0] = (-1.0) ** np.arange(full)
    backward = np.concatenate([real, imag], axis=0) / full
    return np.concatenate(split_table(forward) + split_table(backward), axis=0)


def hyena_kernel(
    dims,
    feats,
    filt_in,
    w_in,
    coef_in,
    tables_in,
    gathered,
    w_all,
    filt_wide,
    filt,
    w_raw,
    wts,
    coef,
    wide_coef,
    spec_hi,
    spec_lo,
    waves,
    tables,
    feat_all,
    filt_all,
    short0,
    carried,
    spec_x,
    spec_f,
    mixed,
    local_sem,
    feat_send,
    feat_recv,
    filt_send,
    filt_recv,
    w_send,
    w_recv,
    wx_send,
    wx_recv,
    x_send,
    x_recv,
    z_send,
    z_recv,
    y_send,
    y_recv,
    s_send,
    s_recv,
):
    ranks, nz, taps = dims
    me = lax.axis_index("ctx")
    core = lax.axis_index("tp")
    x = me % 2
    pair = me // 2
    y = pair % 2
    z = pair // 2
    width = filt_all.shape[1]
    tok = filt_all.shape[2]
    pairs = ranks // 2

    barrier = pltpu.get_barrier_semaphore()

    def greet(d, _):
        pl.semaphore_signal(
            barrier, inc=1, device_id=((me + d) % ranks, core), device_id_type=MESH
        )
        return 0

    lax.fori_loop(1, ranks, greet, 0)
    pl.semaphore_signal(barrier, inc=1, device_id=(me, 1 - core), device_id_type=MESH)
    pl.semaphore_wait(barrier, ranks)

    def remote(src, dst, send, recv, ctx, tp):
        return pltpu.make_async_remote_copy(
            src_ref=src, dst_ref=dst, send_sem=send, recv_sem=recv,
            device_id=(ctx, tp), device_id_type=MESH,
        )

    def feat_copy(d):
        to = (me + d) % ranks
        return remote(
            feats.at[:, pl.ds(to * width, width)], feat_all.at[me],
            feat_send.at[d], feat_recv.at[d], to, core,
        )

    def filt_copy(d):
        to = (me + d) % ranks
        return remote(
            filt.at[pl.ds(to * width, width)], filt_all.at[me],
            filt_send.at[d], filt_recv.at[d], to, core,
        )

    def w_copy(d):
        to = (pair + d) % pairs
        return remote(
            wts.at[to], w_all.at[pair, x], w_send.at[d], w_recv.at[d], to * 2 + x, core
        )

    loads = [
        pltpu.make_async_copy(src, dst, local_sem.at[4 + i])
        for i, (src, dst) in enumerate(
            (
                (filt_in, filt_wide),
                (w_in, w_raw),
                (coef_in, coef),
                (tables_in, tables),
            )
        )
    ]
    for d in range(1, ranks):
        feat_copy(d).start()
    for load in loads:
        load.start()
    own = [
        pltpu.make_async_copy(
            feats.at[:, pl.ds(me * width, width)], feat_all.at[me], local_sem.at[0]
        ),
        pltpu.make_async_copy(filt.at[pl.ds(me * width, width)], filt_all.at[me], local_sem.at[1]),
        pltpu.make_async_copy(wts.at[pair], w_all.at[pair, x], local_sem.at[2]),
    ]
    own[0].start()
    loads[0].wait()
    filt[...] = filt_wide[...].astype(BF16)
    own[1].start()
    for d in range(1, ranks):
        filt_copy(d).start()
    loads[1].wait()
    for i in range(3):
        for h in range(pairs):
            wts[h, :, i * DH : (i + 1) * DH] = w_raw[i, :, h * DH : (h + 1) * DH]
    own[2].start()
    for load in loads[2:]:
        load.wait()
    for i in range(3 * taps + 1):
        wide_coef[i] = jnp.broadcast_to(coef[:, i : i + 1], (width, tok))
    own[0].wait()
    own[1].wait()
    for d in range(1, ranks):
        feat_copy(d).wait_recv()
    for d in range(1, pairs):
        w_copy(d).start()

    lane = lax.broadcasted_iota(jnp.int32, (width, tok), 1)

    def short_block(b, _):
        before = jnp.maximum(b - 1, 0)
        live = jnp.where(b > 0, 1.0, 0.0).astype(F32)
        sums = []
        for i in range(3):
            now = feat_all[b, i].astype(F32)
            past = feat_all[before, i].astype(F32) * live
            total = wide_coef[i] * now
            for lag in range(1, taps):
                moved = pltpu.roll(jnp.where(lane < tok - lag, now, past), lag, 1)
                total = total + wide_coef[lag * 3 + i] * moved
            sums.append(total)
        short0[b] = sums[0]
        carried[b] = (sums[1] * sums[2]).astype(BF16)
        return 0

    lax.fori_loop(0, ranks, short_block, 0)

    group = 4
    fwd_hi = tables.at[pl.ds(0, tok)]
    fwd_lo = tables.at[pl.ds(tok, tok)]
    inv_hi = tables.at[pl.ds(2 * tok, 2 * tok)]
    inv_lo = tables.at[pl.ds(4 * tok, 2 * tok)]

    def spectra(blocks):
        rows = blocks.reshape(group * width, tok)
        spec = jnp.dot(rows, fwd_hi[...], preferred_element_type=F32) + jnp.dot(
            rows, fwd_lo[...], preferred_element_type=F32
        )
        return spec.reshape(group, width, 2 * tok)

    def data_group(g, _):
        here = pl.ds(g * group, group)
        spec_x[here] = spectra(carried[here])
        return 0

    lax.fori_loop(0, ranks // group, data_group, 0)
    for d in range(1, ranks):
        filt_copy(d).wait_recv()

    def filter_group(g, _):
        here = pl.ds(g * group, group)
        spec = spectra(filt_all[here])
        real = spec[:, :, :tok]
        imag = spec[:, :, tok:]
        zero = lax.broadcasted_iota(jnp.int32, imag.shape, 2) == 0
        spec_f[here, 0] = real
        spec_f[here, 1] = jnp.where(zero, 0.0, imag)
        spec_f[here, 2] = jnp.where(zero, imag, real)
        return 0

    lax.fori_loop(0, ranks // group, filter_group, 0)

    def block(m, _):
        def term(d, acc):
            real, imag = acc
            xr = spec_x[m - d, :, :tok]
            xi = spec_x[m - d, :, tok:]
            f_re = spec_f[d, 0]
            f_im = spec_f[d, 1]
            f_ny = spec_f[d, 2]
            return (real + (xr * f_re - xi * f_im), imag + (xr * f_im + xi * f_ny))

        zero = jnp.zeros((width, tok), F32)
        real, imag = lax.fori_loop(0, m + 1, term, (zero, zero))
        rows = pl.ds(pl.multiple_of(m * width, width), width)
        for at, part in enumerate((real, imag)):
            high = part.astype(BF16)
            spec_hi[rows, at * tok : (at + 1) * tok] = high
            spec_lo[rows, at * tok : (at + 1) * tok] = (part - high.astype(F32)).astype(BF16)
        return 0

    lax.fori_loop(0, ranks, block, 0)

    def inverse_group(g, _):
        rows = pl.ds(pl.multiple_of(g * group * width, group * width), group * width)
        high = spec_hi[rows]
        wave = (
            jnp.dot(high, inv_hi[...], preferred_element_type=F32)
            + jnp.dot(spec_lo[rows], inv_hi[...], preferred_element_type=F32)
            + jnp.dot(high, inv_lo[...], preferred_element_type=F32)
        )
        waves[pl.ds(g * group, group)] = wave.reshape(group, width, 2 * tok)
        return 0

    lax.fori_loop(0, ranks // group, inverse_group, 0)

    def finish(m, _):
        live = jnp.where(m > 0, 1.0, 0.0).astype(F32)
        tail = waves[jnp.maximum(m - 1, 0), :, tok:] * live
        long_out = (waves[m, :, :tok] + tail).astype(BF16).astype(F32)
        value = short0[m] * (long_out + wide_coef[3 * taps] * carried[m].astype(F32))
        mixed[m % 2, :, pl.ds(pl.multiple_of((m // 2) * tok, tok), tok)] = value.astype(BF16)
        return 0

    lax.fori_loop(0, ranks, finish, 0)

    keep = pltpu.make_async_copy(mixed.at[x], gathered.at[core, pair, x], local_sem.at[3])
    keep.start()
    swap = remote(
        mixed.at[1 - x], gathered.at[core, pair, x], x_send.at[0], x_recv.at[0],
        pair * 2 + 1 - x, core,
    )
    swap.start()
    keep.wait()
    swap.wait_recv()

    def chunk(p):
        return gathered.at[core, p]

    def up_copy(hop):
        p = (z - hop) * 2 + y
        return remote(
            chunk(p), chunk(p), z_send.at[hop], z_recv.at[hop + 1],
            (z + 1) * 4 + y * 2 + x, core,
        )

    def down_copy(hop):
        p = (z + hop) * 2 + y
        return remote(
            chunk(p), chunk(p), z_send.at[nz + hop], z_recv.at[nz + hop + 1],
            (z - 1) * 4 + y * 2 + x, core,
        )

    def y_copy(origin):
        p = origin * 2 + y
        return remote(
            chunk(p), chunk(p), y_send.at[origin], y_recv.at[origin],
            z * 4 + (1 - y) * 2 + x, core,
        )

    def s_copy(origin, side):
        p = origin * 2 + jnp.where(side == 0, y, 1 - y)
        return remote(
            chunk(p), chunk(p), s_send.at[side * nz + origin], s_recv.at[side * nz + origin],
            me, 1 - core,
        )

    def arrived(hop, up):
        p = (z - hop if up else z + hop) * 2 + y
        at = hop if up else nz + hop
        remote(
            chunk(p), chunk(p), z_send.at[0], z_recv.at[at],
            (z - 1 if up else z + 1) * 4 + y * 2 + x, core,
        ).wait_recv()

    @pl.when(z < nz - 1)
    def _():
        up_copy(0).start()

    @pl.when(z > 0)
    def _():
        down_copy(0).start()

    y_copy(z).start()
    s_copy(z, 0).start()

    own[2].wait()
    for d in range(1, pairs):
        w_copy(d).wait_recv()
    w_swap = remote(
        w_all.at[:, x], w_all.at[:, x], wx_send.at[0], wx_recv.at[0], pair * 2 + 1 - x, core
    )
    w_swap.start()

    for hop in range(1, nz):

        @pl.when(z - hop >= 0)
        def _():
            arrived(hop, True)

            @pl.when(z < nz - 1)
            def _():
                up_copy(hop).start()

            y_copy(z - hop).start()
            s_copy(z - hop, 0).start()

        @pl.when(z + hop < nz)
        def _():
            arrived(hop, False)

            @pl.when(z > 0)
            def _():
                down_copy(hop).start()

            y_copy(z + hop).start()
            s_copy(z + hop, 0).start()

    for hop in range(nz):

        @pl.when(z - hop >= 0)
        def _():
            y_copy(z - hop).wait_recv()
            s_copy(z - hop, 1).start()

        if hop > 0:

            @pl.when(z + hop < nz)
            def _():
                y_copy(z + hop).wait_recv()
                s_copy(z + hop, 1).start()

    for origin in range(nz):
        s_copy(origin, 0).wait_recv()
        s_copy(origin, 1).wait_recv()
    w_swap.wait()
    for d in range(1, ranks):
        feat_copy(d).wait_send()
        filt_copy(d).wait_send()
    for d in range(1, pairs):
        w_copy(d).wait_send()
    swap.wait_send()
    for hop in range(nz):

        @pl.when((z < nz - 1) & (z - hop >= 0))
        def _():
            up_copy(hop).wait_send()

        @pl.when((z > 0) & (z + hop < nz))
        def _():
            down_copy(hop).wait_send()

    for origin in range(nz):
        y_copy(origin).wait_send()
        s_copy(origin, 0).wait_send()
        s_copy(origin, 1).wait_send()


def hyena(features, filt, w_qkv, coef, nz, taps):
    ranks = features.shape[1] // coef.shape[0]
    width = coef.shape[0]
    tok = features.shape[2]
    pairs = ranks // 2
    rows = w_qkv.shape[1]
    columns = 3 * DH
    tables = jnp.asarray(packed_tables(tok))
    hbm = pl.BlockSpec(memory_space=pl.ANY)
    dma = pltpu.SemaphoreType.DMA
    return pl.pallas_call(
        functools.partial(hyena_kernel, (ranks, nz, taps)),
        out_shape=(
            jax.ShapeDtypeStruct((2, pairs, 2, width, pairs * tok), BF16),
            jax.ShapeDtypeStruct((pairs, 2, rows, columns), BF16),
        ),
        in_specs=[hbm] * 5,
        out_specs=(hbm, hbm),
        scratch_shapes=[
            pltpu.VMEM(filt.shape, F32),
            pltpu.VMEM(filt.shape, BF16),
            pltpu.VMEM(w_qkv.shape, BF16),
            pltpu.VMEM((pairs, rows, columns), BF16),
            pltpu.VMEM(coef.shape, F32),
            pltpu.VMEM((3 * taps + 1, width, tok), F32),
            pltpu.VMEM((ranks * width, 2 * tok), BF16),
            pltpu.VMEM((ranks * width, 2 * tok), BF16),
            pltpu.VMEM((ranks, width, 2 * tok), F32),
        ]
        + [pltpu.VMEM(tables.shape, BF16)]
        + [
            pltpu.VMEM((ranks, 3, width, tok), BF16),
            pltpu.VMEM((ranks, width, tok), BF16),
            pltpu.VMEM((ranks, width, tok), F32),
            pltpu.VMEM((ranks, width, tok), BF16),
            pltpu.VMEM((ranks, width, 2 * tok), F32),
            pltpu.VMEM((ranks, 3, width, tok), F32),
            pltpu.VMEM((2, width, pairs * tok), BF16),
            dma((8,)),
            dma((ranks,)),
            dma((ranks,)),
            dma((ranks,)),
            dma((ranks,)),
            dma((pairs,)),
            dma((pairs,)),
            dma((1,)),
            dma((1,)),
            dma((1,)),
            dma((1,)),
            dma((2 * nz,)),
            dma((2 * nz,)),
            dma((nz,)),
            dma((nz,)),
            dma((2 * nz,)),
            dma((2 * nz,)),
        ],
        compiler_params=pltpu.CompilerParams(
            collective_id=0, has_side_effects=True, vmem_limit_bytes=60 * 2**20
        ),
    )(features, filt, w_qkv, coef, tables)


def attend_kernel(
    pairs, tok, proj, out, other, top, total, accum, result,
    local_sem, kv_send, kv_recv, send, recv,
):
    me = lax.axis_index("ctx")
    core = lax.axis_index("tp")
    x = me % 2
    pair = me // 2
    parts = kv_send.shape[0]
    rows = pairs * tok // parts
    scale = DH ** (-0.5)

    barrier = pltpu.get_barrier_semaphore()
    for d in range(1, pairs):
        to = (pair + d) % pairs
        pl.semaphore_signal(barrier, inc=1, device_id=(to * 2 + x, core), device_id_type=MESH)
    pl.semaphore_signal(
        barrier, inc=1, device_id=(pair * 2 + 1 - x, core), device_id_type=MESH
    )
    pl.semaphore_wait(barrier, pairs)

    def kv_copy(c):
        return pltpu.make_async_remote_copy(
            src_ref=proj.at[pl.ds(c * rows, rows), pl.ds(DH, 2 * DH)],
            dst_ref=other.at[pl.ds(c * rows, rows)],
            send_sem=kv_send.at[c], recv_sem=kv_recv.at[c],
            device_id=(pair * 2 + 1 - x, core), device_id_type=MESH,
        )

    for c in range(parts):
        kv_copy(c).start()

    def dot_t(a, b):
        return lax.dot_general(a, b, (((1,), (1,)), ((), ())), preferred_element_type=F32)

    for j in range(pairs):
        here = pl.ds(j * tok, tok)
        count = (j + 1) * tok
        scores = dot_t(proj[here, :DH], proj[:count, DH : 2 * DH]) * scale
        col = lax.broadcasted_iota(jnp.int32, (tok, count), 1)
        row = lax.broadcasted_iota(jnp.int32, (tok, count), 0)
        scores = jnp.where(col <= row + j * tok, scores, -1e30)
        peak = jnp.max(scores, axis=1, keepdims=True)
        expo = jnp.exp(scores - peak)
        top[here] = jnp.broadcast_to(peak, (tok, DH))
        total[here] = jnp.broadcast_to(jnp.sum(expo, axis=1, keepdims=True), (tok, DH))
        accum[here] = jnp.dot(
            expo.astype(BF16), proj[:count, 2 * DH :], preferred_element_type=F32
        )

    def back_copy(j):
        return pltpu.make_async_remote_copy(
            src_ref=result.at[j], dst_ref=out.at[:, pl.ds(pl.multiple_of(pair * DH, DH), DH)],
            send_sem=send.at[j], recv_sem=recv.at[pair],
            device_id=(j * 2 + x, core), device_id_type=MESH,
        )

    for j in range(pairs):
        here = pl.ds(j * tok, tok)
        count = (j + 1) * tok
        if j * tok % rows == 0:
            kv_copy(j * tok // rows).wait_recv()
        scores = dot_t(proj[here, :DH], other[:count, :DH]) * scale
        col = lax.broadcasted_iota(jnp.int32, (tok, count), 1)
        scores = jnp.where(col < (j + x) * tok, scores, -1e30)
        peak = top[here]
        new_peak = jnp.maximum(peak, jnp.max(scores, axis=1, keepdims=True))
        factor = jnp.exp(peak - new_peak)
        expo = jnp.exp(scores - new_peak[:, :1])
        summed = total[here] * factor + jnp.sum(expo, axis=1, keepdims=True)
        value = accum[here] * factor + jnp.dot(
            expo.astype(BF16), other[:count, DH:], preferred_element_type=F32
        )
        result[j] = (value / summed).astype(BF16)

        @pl.when(j != pair)
        def _():
            back_copy(j).start()

    own = pltpu.make_async_copy(
        result.at[pair], out.at[:, pl.ds(pl.multiple_of(pair * DH, DH), DH)], local_sem
    )
    own.start()
    own.wait()
    for c in range(parts):
        kv_copy(c).wait_send()
    for j in range(pairs):

        @pl.when(j != pair)
        def _():
            back_copy(j).wait_send()

    for d in range(1, pairs):
        frm = (pair + d) % pairs
        pltpu.make_async_remote_copy(
            src_ref=result.at[frm],
            dst_ref=out.at[:, pl.ds(pl.multiple_of(frm * DH, DH), DH)],
            send_sem=send.at[frm], recv_sem=recv.at[frm],
            device_id=(frm * 2 + x, core), device_id_type=MESH,
        ).wait_recv()


def attend(projected, pairs, tok):
    vmem = pl.BlockSpec(memory_space=pltpu.VMEM)
    dma = pltpu.SemaphoreType.DMA
    rows = pairs * tok
    parts = 4
    return pl.pallas_call(
        functools.partial(attend_kernel, pairs, tok),
        out_shape=jax.ShapeDtypeStruct((tok, pairs * DH), BF16),
        in_specs=[vmem],
        out_specs=vmem,
        scratch_shapes=[
            pltpu.VMEM((rows, 2 * DH), BF16),
            pltpu.VMEM((rows, DH), F32),
            pltpu.VMEM((rows, DH), F32),
            pltpu.VMEM((rows, DH), F32),
            pltpu.VMEM((pairs, tok, DH), BF16),
            dma,
            dma((parts,)),
            dma((parts,)),
            dma((pairs,)),
            dma((pairs,)),
        ],
        compiler_params=pltpu.CompilerParams(
            collective_id=1, has_side_effects=True, vmem_limit_bytes=32 * 2**20
        ),
    )(projected)


def local_pairs(features, short_taps, long_filter, skip, norm_gain, w_qkv):
    ranks = lax.axis_size("ctx")
    pairs = ranks // 2
    me = lax.axis_index("ctx")
    core = lax.axis_index("tp")
    x = me % 2
    taps = short_taps.shape[0]
    tok = features.shape[2]
    width = features.shape[1] // ranks
    taps_here = lax.dynamic_slice_in_dim(short_taps, me * width, width, 2)
    skip_here = lax.dynamic_slice_in_dim(skip, me * width, width, 0)
    coef = jnp.concatenate([taps_here.reshape(taps * 3, width), skip_here[None]], axis=0).T
    coef = jnp.pad(coef, ((0, 0), (0, DH - coef.shape[1])))
    stacked = jnp.transpose(w_qkv, (1, 0, 2))
    gathered, w_all = hyena(features, long_filter, stacked, coef, ranks // 4, taps)
    channels = norm_gain.shape[0]
    whole = gathered.reshape(channels, pairs * tok)
    half = lax.dynamic_slice(
        gathered,
        (core, 0, 0, 0, (me // 2) * tok),
        (1, pairs, 2, width, tok),
    ).reshape(channels // 2, tok)
    whole_f = whole.astype(F32)
    inverse = lax.rsqrt(jnp.mean(whole_f * whole_f, axis=0, keepdims=True) + 1e-06)
    normed = (whole_f * inverse * norm_gain[:, None]).astype(BF16)
    projected = lax.dot_general(
        normed, w_all.reshape(channels, 3 * DH), (((0,), (0,)), ((), ())),
        preferred_element_type=F32,
    ).astype(BF16)
    attended = attend(projected, pairs, tok)
    return (half, attended)


def solution(mesh):
    in_specs = (
        P(None, "tp", "ctx"),
        P(None, None, "tp"),
        P("tp", "ctx"),
        P("tp"),
        P(),
        P("ctx", None, "tp"),
    )
    out_specs = (P("tp", "ctx"), P("ctx", "tp"))

    def whole(features, short_taps, long_filter, skip, norm_gain, w_qkv):
        heads = w_qkv.shape[2] // mesh.shape["tp"] // DH
        paired = mesh.shape["ctx"] == 16 and heads == 8
        body = local_pairs if paired else local
        return jax.shard_map(
            body, mesh=mesh, in_specs=in_specs, out_specs=out_specs, check_vma=False
        )(features, short_taps, long_filter, skip, norm_gain, w_qkv)

    return whole
```

```python
import functools
import math

import jax
import jax.numpy as jnp
import ml_dtypes
import numpy as np
from jax import lax
from jax.experimental import pallas as pl
from jax.experimental.pallas import tpu as pltpu
from jax.sharding import PartitionSpec as P

DH = 128


HIGHEST = lax.Precision.HIGHEST


def shifted(block, axis, distance):
    devices = range(lax.axis_size(axis))
    route = [(i - distance, i) for i in devices if i - distance in devices]
    return lax.ppermute(block, axis, route)


def angle_table(rows, cols, modulus):
    left = jnp.arange(rows, dtype=jnp.int32)[:, None]
    right = jnp.arange(cols, dtype=jnp.int32)[None, :]
    phase = (left * right % modulus).astype(jnp.float32) * (2.0 * math.pi / modulus)
    return (jnp.cos(phase), jnp.sin(phase))


def contract(form, data, table):
    return jnp.einsum(form, data, table, precision=HIGHEST)


def spectrum(lanes, tok):
    width = lanes.shape[0]
    length = lanes.shape[1]
    outer = 2 * tok
    inner = 2 * length // outer
    data = lanes.reshape(width, tok, inner)
    cos_a, sin_a = angle_table(tok, outer, outer)
    first_re = contract("kaq,ab->kbq", data, cos_a)
    first_im = -contract("kaq,ab->kbq", data, sin_a)
    cos_t, sin_t = angle_table(outer, inner, 2 * length)
    turned_re = first_re * cos_t + first_im * sin_t
    turned_im = first_im * cos_t - first_re * sin_t
    cos_b, sin_b = angle_table(inner, inner, inner)
    out_re = contract("kbq,qr->kbr", turned_re, cos_b) + contract("kbq,qr->kbr", turned_im, sin_b)
    out_im = contract("kbq,qr->kbr", turned_im, cos_b) - contract("kbq,qr->kbr", turned_re, sin_b)
    return (out_re, out_im)


def inverse_real(spec_re, spec_im, tok, length):
    width = spec_re.shape[0]
    outer = 2 * tok
    inner = spec_re.shape[2]
    cos_b, sin_b = angle_table(inner, inner, inner)
    back_re = contract("kbr,rq->kbq", spec_re, cos_b) - contract("kbr,rq->kbq", spec_im, sin_b)
    back_im = contract("kbr,rq->kbq", spec_im, cos_b) + contract("kbr,rq->kbq", spec_re, sin_b)
    cos_t, sin_t = angle_table(outer, inner, 2 * length)
    turned_re = back_re * cos_t - back_im * sin_t
    turned_im = back_im * cos_t + back_re * sin_t
    cos_a, sin_a = angle_table(outer, tok, outer)
    real = contract("kbq,ba->kaq", turned_re, cos_a) - contract("kbq,ba->kaq", turned_im, sin_a)
    return (real / (2 * length)).reshape(width, length)


def attend_rows(query_rows, query_pos, keyvals, count, block):
    rows = query_rows.shape[0]
    scale = DH ** (-0.5)
    start_state = (
        jnp.full((rows,), -1e30, jnp.float32),
        jnp.zeros((rows,), jnp.float32),
        jnp.zeros((rows, DH), jnp.float32),
    )

    def step(index, state):
        running, total, accum = state
        part = lax.dynamic_slice_in_dim(keyvals, index * block, block, 0)
        keys = part[:, :DH]
        vals = part[:, DH:]
        scores = (
            lax.dot_general(
                query_rows, keys, (((1,), (1,)), ((), ())), preferred_element_type=jnp.float32
            )
            * scale
        )
        key_pos = index * block + jnp.arange(block, dtype=jnp.int32)
        allowed = key_pos[None, :] <= query_pos[:, None]
        scores = jnp.where(allowed, scores, -1e30)
        new_top = jnp.maximum(running, jnp.max(scores, axis=1))
        factor = jnp.exp(running - new_top)
        expo = jnp.where(allowed, jnp.exp(scores - new_top[:, None]), 0.0)
        total = total * factor + jnp.sum(expo, axis=1)
        accum = accum * factor[:, None] + jnp.dot(
            expo.astype(jnp.bfloat16), vals, preferred_element_type=jnp.float32
        )
        return (new_top, total, accum)

    running, total, accum = lax.fori_loop(0, count, step, start_state)
    return accum / total[:, None]


def local(features, short_taps, long_filter, skip, norm_gain, w_qkv):
    taps = short_taps.shape[0]
    tok = features.shape[2]
    rim = shifted(features[:, :, tok - (taps - 1) :], "ctx", 1)
    extended = jnp.concatenate([rim, features], axis=2).astype(jnp.float32)
    short = short_taps[0][:, :, None] * extended[:, :, taps - 1 : taps - 1 + tok]
    for lag in range(1, taps):
        short = (
            short
            + short_taps[lag][:, :, None] * extended[:, :, taps - 1 - lag : taps - 1 - lag + tok]
        )
    carried = (short[1] * short[2]).astype(jnp.bfloat16)
    lanes = lax.all_to_all(carried, "ctx", split_axis=0, concat_axis=1, tiled=True).astype(
        jnp.float32
    )
    filt = lax.all_to_all(long_filter, "ctx", split_axis=0, concat_axis=1, tiled=True)
    length = lanes.shape[1]
    data_re, data_im = spectrum(lanes, tok)
    filt_re, filt_im = spectrum(filt, tok)
    conv = inverse_real(
        data_re * filt_re - data_im * filt_im, data_re * filt_im + data_im * filt_re, tok, length
    )
    long_back = lax.all_to_all(
        conv.astype(jnp.bfloat16), "ctx", split_axis=1, concat_axis=0, tiled=True
    )
    mixed = (
        short[0] * (long_back.astype(jnp.float32) + skip[:, None] * carried.astype(jnp.float32))
    ).astype(jnp.bfloat16)
    whole = lax.all_gather(mixed, "tp", axis=0, tiled=True)
    whole_f = whole.astype(jnp.float32)
    inverse = lax.rsqrt(jnp.mean(whole_f * whole_f, axis=0, keepdims=True) + 1e-06)
    normed = (whole_f * inverse * norm_gain[:, None]).astype(jnp.bfloat16)
    columns = w_qkv.shape[1] * w_qkv.shape[2]
    piece = lax.all_gather(w_qkv, "ctx", axis=0, tiled=True)
    count = piece.shape[0]
    projected = lax.dot_general(
        normed,
        piece.reshape(count, columns),
        (((0,), (0,)), ((), ())),
        preferred_element_type=jnp.float32,
    )
    heads = w_qkv.shape[2] // DH
    projected = projected.astype(jnp.bfloat16).reshape(tok, 3, heads, DH)
    ranks = lax.axis_size("ctx")
    subs = ranks // heads
    sub = tok // subs
    key_pairs = jnp.concatenate([projected[:, 1], projected[:, 2]], axis=-1)
    slot = lax.axis_index("ctx") % subs
    queries = jnp.transpose(projected[:, 0].reshape(subs, sub, heads, DH), (2, 0, 1, 3)).reshape(
        ranks, sub, DH
    )
    pairs = jnp.transpose(key_pairs, (1, 0, 2))
    pairs = jnp.broadcast_to(pairs[:, None], (heads, subs, tok, 2 * DH)).reshape(ranks, tok, 2 * DH)
    got_queries = lax.all_to_all(queries, "ctx", split_axis=0, concat_axis=0, tiled=True).reshape(
        ranks * sub, DH
    )
    got_pairs = lax.all_to_all(pairs, "ctx", split_axis=0, concat_axis=0, tiled=True).reshape(
        ranks * tok, 2 * DH
    )
    source = jnp.arange(ranks * sub, dtype=jnp.int32)
    query_pos = source // sub * tok + slot * sub + source % sub
    total_keys = ranks * tok
    block = min(2048, total_keys)
    result = attend_rows(got_queries, query_pos, got_pairs, total_keys // block, block)
    result = result.astype(jnp.bfloat16).reshape(ranks, sub, DH)
    back = lax.all_to_all(result, "ctx", split_axis=0, concat_axis=0, tiled=True)
    attended = jnp.transpose(back.reshape(heads, subs, sub, DH), (1, 2, 0, 3)).reshape(
        tok, heads * DH
    )
    return (mixed, attended)


MESH = pl.DeviceIdType.MESH
F32 = jnp.float32
BF16 = jnp.bfloat16


def split_table(table):
    high = table.astype(ml_dtypes.bfloat16)
    low = (table - high.astype(np.float64)).astype(ml_dtypes.bfloat16)
    return [high, low]


def packed_tables(tok):
    full = 2 * tok
    pos = np.arange(tok)[:, None]
    freq = np.arange(tok)[None, :]
    angle = 2.0 * np.pi * ((pos * freq) % full) / full
    imag = -np.sin(angle)
    imag[:, 0] = (-1.0) ** np.arange(tok)
    forward = np.concatenate([np.cos(angle), imag], axis=1)
    out = np.arange(full)[None, :]
    freq = np.arange(tok)[:, None]
    angle = 2.0 * np.pi * ((out * freq) % full) / full
    real = 2.0 * np.cos(angle)
    real[0] = 1.0
    imag = -2.0 * np.sin(angle)
    imag[0] = (-1.0) ** np.arange(full)
    backward = np.concatenate([real, imag], axis=0) / full
    return np.concatenate(split_table(forward) + split_table(backward), axis=0)


def hyena_kernel(
    dims,
    feats,
    filt_in,
    w_in,
    coef_in,
    tables_in,
    gathered,
    w_all,
    filt_wide,
    filt,
    w_raw,
    wts,
    coef,
    wide_coef,
    spec_hi,
    spec_lo,
    waves,
    tables,
    feat_all,
    filt_all,
    short0,
    carried,
    spec_x,
    spec_f,
    mixed,
    local_sem,
    feat_send,
    feat_recv,
    filt_send,
    filt_recv,
    w_send,
    w_recv,
    wx_send,
    wx_recv,
    x_send,
    x_recv,
    z_send,
    z_recv,
    y_send,
    y_recv,
    s_send,
    s_recv,
):
    ranks, nz, taps = dims
    me = lax.axis_index("ctx")
    core = lax.axis_index("tp")
    x = me % 2
    pair = me // 2
    y = pair % 2
    z = pair // 2
    width = filt_all.shape[1]
    tok = filt_all.shape[2]
    pairs = ranks // 2

    barrier = pltpu.get_barrier_semaphore()

    def greet(d, _):
        pl.semaphore_signal(
            barrier, inc=1, device_id=((me + d) % ranks, core), device_id_type=MESH
        )
        return 0

    lax.fori_loop(1, ranks, greet, 0)
    pl.semaphore_signal(barrier, inc=1, device_id=(me, 1 - core), device_id_type=MESH)
    pl.semaphore_wait(barrier, ranks)

    def remote(src, dst, send, recv, ctx, tp):
        return pltpu.make_async_remote_copy(
            src_ref=src, dst_ref=dst, send_sem=send, recv_sem=recv,
            device_id=(ctx, tp), device_id_type=MESH,
        )

    def feat_copy(d):
        to = (me + d) % ranks
        return remote(
            feats.at[:, pl.ds(to * width, width)], feat_all.at[me],
            feat_send.at[d], feat_recv.at[d], to, core,
        )

    def filt_copy(d):
        to = (me + d) % ranks
        return remote(
            filt.at[pl.ds(to * width, width)], filt_all.at[me],
            filt_send.at[d], filt_recv.at[d], to, core,
        )

    def w_copy(d):
        to = (pair + d) % pairs
        return remote(
            wts.at[to], w_all.at[pair, x], w_send.at[d], w_recv.at[d], to * 2 + x, core
        )

    loads = [
        pltpu.make_async_copy(src, dst, local_sem.at[4 + i])
        for i, (src, dst) in enumerate(
            (
                (filt_in, filt_wide),
                (w_in, w_raw),
                (coef_in, coef),
                (tables_in, tables),
            )
        )
    ]
    for d in range(1, ranks):
        feat_copy(d).start()
    for load in loads:
        load.start()
    own = [
        pltpu.make_async_copy(
            feats.at[:, pl.ds(me * width, width)], feat_all.at[me], local_sem.at[0]
        ),
        pltpu.make_async_copy(filt.at[pl.ds(me * width, width)], filt_all.at[me], local_sem.at[1]),
        pltpu.make_async_copy(wts.at[pair], w_all.at[pair, x], local_sem.at[2]),
    ]
    own[0].start()
    loads[0].wait()
    filt[...] = filt_wide[...].astype(BF16)
    own[1].start()
    for d in range(1, ranks):
        filt_copy(d).start()
    loads[1].wait()
    for i in range(3):
        for h in range(pairs):
            wts[h, :, i * DH : (i + 1) * DH] = w_raw[i, :, h * DH : (h + 1) * DH]
    own[2].start()
    for load in loads[2:]:
        load.wait()
    for i in range(3 * taps + 1):
        wide_coef[i] = jnp.broadcast_to(coef[:, i : i + 1], (width, tok))
    own[0].wait()
    own[1].wait()
    for d in range(1, ranks):
        feat_copy(d).wait_recv()
    for d in range(1, pairs):
        w_copy(d).start()

    lane = lax.broadcasted_iota(jnp.int32, (width, tok), 1)

    def short_block(b, _):
        before = jnp.maximum(b - 1, 0)
        live = jnp.where(b > 0, 1.0, 0.0).astype(F32)
        sums = []
        for i in range(3):
            now = feat_all[b, i].astype(F32)
            past = feat_all[before, i].astype(F32) * live
            total = wide_coef[i] * now
            for lag in range(1, taps):
                moved = pltpu.roll(jnp.where(lane < tok - lag, now, past), lag, 1)
                total = total + wide_coef[lag * 3 + i] * moved
            sums.append(total)
        short0[b] = sums[0]
        carried[b] = (sums[1] * sums[2]).astype(BF16)
        return 0

    lax.fori_loop(0, ranks, short_block, 0)

    group = 4
    fwd_hi = tables.at[pl.ds(0, tok)]
    fwd_lo = tables.at[pl.ds(tok, tok)]
    inv_hi = tables.at[pl.ds(2 * tok, 2 * tok)]
    inv_lo = tables.at[pl.ds(4 * tok, 2 * tok)]

    def spectra(blocks):
        rows = blocks.reshape(group * width, tok)
        spec = jnp.dot(rows, fwd_hi[...], preferred_element_type=F32) + jnp.dot(
            rows, fwd_lo[...], preferred_element_type=F32
        )
        return spec.reshape(group, width, 2 * tok)

    def data_group(g, _):
        here = pl.ds(g * group, group)
        spec_x[here] = spectra(carried[here])
        return 0

    lax.fori_loop(0, ranks // group, data_group, 0)
    for d in range(1, ranks):
        filt_copy(d).wait_recv()

    def filter_group(g, _):
        here = pl.ds(g * group, group)
        spec = spectra(filt_all[here])
        real = spec[:, :, :tok]
        imag = spec[:, :, tok:]
        zero = lax.broadcasted_iota(jnp.int32, imag.shape, 2) == 0
        spec_f[here, 0] = real
        spec_f[here, 1] = jnp.where(zero, 0.0, imag)
        spec_f[here, 2] = jnp.where(zero, imag, real)
        return 0

    lax.fori_loop(0, ranks // group, filter_group, 0)

    def block(m, _):
        def term(d, acc):
            real, imag = acc
            xr = spec_x[m - d, :, :tok]
            xi = spec_x[m - d, :, tok:]
            f_re = spec_f[d, 0]
            f_im = spec_f[d, 1]
            f_ny = spec_f[d, 2]
            return (real + (xr * f_re - xi * f_im), imag + (xr * f_im + xi * f_ny))

        zero = jnp.zeros((width, tok), F32)
        real, imag = lax.fori_loop(0, m + 1, term, (zero, zero))
        rows = pl.ds(pl.multiple_of(m * width, width), width)
        for at, part in enumerate((real, imag)):
            high = part.astype(BF16)
            spec_hi[rows, at * tok : (at + 1) * tok] = high
            spec_lo[rows, at * tok : (at + 1) * tok] = (part - high.astype(F32)).astype(BF16)
        return 0

    lax.fori_loop(0, ranks, block, 0)

    def inverse_group(g, _):
        rows = pl.ds(pl.multiple_of(g * group * width, group * width), group * width)
        high = spec_hi[rows]
        wave = (
            jnp.dot(high, inv_hi[...], preferred_element_type=F32)
            + jnp.dot(spec_lo[rows], inv_hi[...], preferred_element_type=F32)
            + jnp.dot(high, inv_lo[...], preferred_element_type=F32)
        )
        waves[pl.ds(g * group, group)] = wave.reshape(group, width, 2 * tok)
        return 0

    lax.fori_loop(0, ranks // group, inverse_group, 0)

    def finish(m, _):
        live = jnp.where(m > 0, 1.0, 0.0).astype(F32)
        tail = waves[jnp.maximum(m - 1, 0), :, tok:] * live
        long_out = (waves[m, :, :tok] + tail).astype(BF16).astype(F32)
        value = short0[m] * (long_out + wide_coef[3 * taps] * carried[m].astype(F32))
        mixed[m % 2, :, pl.ds(pl.multiple_of((m // 2) * tok, tok), tok)] = value.astype(BF16)
        return 0

    lax.fori_loop(0, ranks, finish, 0)

    keep = pltpu.make_async_copy(mixed.at[x], gathered.at[core, pair, x], local_sem.at[3])
    keep.start()
    swap = remote(
        mixed.at[1 - x], gathered.at[core, pair, x], x_send.at[0], x_recv.at[0],
        pair * 2 + 1 - x, core,
    )
    swap.start()
    keep.wait()
    swap.wait_recv()

    def chunk(p):
        return gathered.at[core, p]

    def up_copy(hop):
        p = (z - hop) * 2 + y
        return remote(
            chunk(p), chunk(p), z_send.at[hop], z_recv.at[hop + 1],
            (z + 1) * 4 + y * 2 + x, core,
        )

    def down_copy(hop):
        p = (z + hop) * 2 + y
        return remote(
            chunk(p), chunk(p), z_send.at[nz + hop], z_recv.at[nz + hop + 1],
            (z - 1) * 4 + y * 2 + x, core,
        )

    def y_copy(origin):
        p = origin * 2 + y
        return remote(
            chunk(p), chunk(p), y_send.at[origin], y_recv.at[origin],
            z * 4 + (1 - y) * 2 + x, core,
        )

    def s_copy(origin, side):
        p = origin * 2 + jnp.where(side == 0, y, 1 - y)
        return remote(
            chunk(p), chunk(p), s_send.at[side * nz + origin], s_recv.at[side * nz + origin],
            me, 1 - core,
        )

    def arrived(hop, up):
        p = (z - hop if up else z + hop) * 2 + y
        at = hop if up else nz + hop
        remote(
            chunk(p), chunk(p), z_send.at[0], z_recv.at[at],
            (z - 1 if up else z + 1) * 4 + y * 2 + x, core,
        ).wait_recv()

    @pl.when(z < nz - 1)
    def _():
        up_copy(0).start()

    @pl.when(z > 0)
    def _():
        down_copy(0).start()

    y_copy(z).start()
    s_copy(z, 0).start()

    for hop in range(1, nz):
        if hop == 2:
            own[2].wait()
            for d in range(1, pairs):
                w_copy(d).wait_recv()
            w_swap = remote(
                w_all.at[:, x], w_all.at[:, x], wx_send.at[0], wx_recv.at[0], pair * 2 + 1 - x, core
            )
            w_swap.start()

        @pl.when(z - hop >= 0)
        def _():
            arrived(hop, True)

            @pl.when(z < nz - 1)
            def _():
                up_copy(hop).start()

            y_copy(z - hop).start()
            s_copy(z - hop, 0).start()

        @pl.when(z + hop < nz)
        def _():
            arrived(hop, False)

            @pl.when(z > 0)
            def _():
                down_copy(hop).start()

            y_copy(z + hop).start()
            s_copy(z + hop, 0).start()

    for hop in range(nz):

        @pl.when(z - hop >= 0)
        def _():
            y_copy(z - hop).wait_recv()
            s_copy(z - hop, 1).start()

        if hop > 0:

            @pl.when(z + hop < nz)
            def _():
                y_copy(z + hop).wait_recv()
                s_copy(z + hop, 1).start()

    for origin in range(nz):
        s_copy(origin, 0).wait_recv()
        s_copy(origin, 1).wait_recv()
    w_swap.wait()
    for d in range(1, ranks):
        feat_copy(d).wait_send()
        filt_copy(d).wait_send()
    for d in range(1, pairs):
        w_copy(d).wait_send()
    swap.wait_send()
    for hop in range(nz):

        @pl.when((z < nz - 1) & (z - hop >= 0))
        def _():
            up_copy(hop).wait_send()

        @pl.when((z > 0) & (z + hop < nz))
        def _():
            down_copy(hop).wait_send()

    for origin in range(nz):
        y_copy(origin).wait_send()
        s_copy(origin, 0).wait_send()
        s_copy(origin, 1).wait_send()


def hyena(features, filt, w_qkv, coef, nz, taps):
    ranks = features.shape[1] // coef.shape[0]
    width = coef.shape[0]
    tok = features.shape[2]
    pairs = ranks // 2
    rows = w_qkv.shape[1]
    columns = 3 * DH
    tables = jnp.asarray(packed_tables(tok))
    hbm = pl.BlockSpec(memory_space=pl.ANY)
    dma = pltpu.SemaphoreType.DMA
    return pl.pallas_call(
        functools.partial(hyena_kernel, (ranks, nz, taps)),
        out_shape=(
            jax.ShapeDtypeStruct((2, pairs, 2, width, pairs * tok), BF16),
            jax.ShapeDtypeStruct((pairs, 2, rows, columns), BF16),
        ),
        in_specs=[hbm] * 5,
        out_specs=(hbm, hbm),
        scratch_shapes=[
            pltpu.VMEM(filt.shape, F32),
            pltpu.VMEM(filt.shape, BF16),
            pltpu.VMEM(w_qkv.shape, BF16),
            pltpu.VMEM((pairs, rows, columns), BF16),
            pltpu.VMEM(coef.shape, F32),
            pltpu.VMEM((3 * taps + 1, width, tok), F32),
            pltpu.VMEM((ranks * width, 2 * tok), BF16),
            pltpu.VMEM((ranks * width, 2 * tok), BF16),
            pltpu.VMEM((ranks, width, 2 * tok), F32),
        ]
        + [pltpu.VMEM(tables.shape, BF16)]
        + [
            pltpu.VMEM((ranks, 3, width, tok), BF16),
            pltpu.VMEM((ranks, width, tok), BF16),
            pltpu.VMEM((ranks, width, tok), F32),
            pltpu.VMEM((ranks, width, tok), BF16),
            pltpu.VMEM((ranks, width, 2 * tok), F32),
            pltpu.VMEM((ranks, 3, width, tok), F32),
            pltpu.VMEM((2, width, pairs * tok), BF16),
            dma((8,)),
            dma((ranks,)),
            dma((ranks,)),
            dma((ranks,)),
            dma((ranks,)),
            dma((pairs,)),
            dma((pairs,)),
            dma((1,)),
            dma((1,)),
            dma((1,)),
            dma((1,)),
            dma((2 * nz,)),
            dma((2 * nz,)),
            dma((nz,)),
            dma((nz,)),
            dma((2 * nz,)),
            dma((2 * nz,)),
        ],
        compiler_params=pltpu.CompilerParams(
            collective_id=0, has_side_effects=True, vmem_limit_bytes=60 * 2**20
        ),
    )(features, filt, w_qkv, coef, tables)


def attend_kernel(
    pairs, tok, proj, out, other, top, total, accum, result,
    local_sem, kv_send, kv_recv, send, recv,
):
    me = lax.axis_index("ctx")
    core = lax.axis_index("tp")
    x = me % 2
    pair = me // 2
    parts = kv_send.shape[0]
    rows = pairs * tok // parts
    scale = DH ** (-0.5)

    barrier = pltpu.get_barrier_semaphore()
    for d in range(1, pairs):
        to = (pair + d) % pairs
        pl.semaphore_signal(barrier, inc=1, device_id=(to * 2 + x, core), device_id_type=MESH)
    pl.semaphore_signal(
        barrier, inc=1, device_id=(pair * 2 + 1 - x, core), device_id_type=MESH
    )
    pl.semaphore_wait(barrier, pairs)

    def kv_copy(c):
        return pltpu.make_async_remote_copy(
            src_ref=proj.at[pl.ds(c * rows, rows), pl.ds(DH, 2 * DH)],
            dst_ref=other.at[pl.ds(c * rows, rows)],
            send_sem=kv_send.at[c], recv_sem=kv_recv.at[c],
            device_id=(pair * 2 + 1 - x, core), device_id_type=MESH,
        )

    for c in range(parts):
        kv_copy(c).start()

    def dot_t(a, b):
        return lax.dot_general(a, b, (((1,), (1,)), ((), ())), preferred_element_type=F32)

    for j in range(pairs):
        here = pl.ds(j * tok, tok)
        count = (j + 1) * tok
        scores = dot_t(proj[here, :DH], proj[:count, DH : 2 * DH]) * scale
        col = lax.broadcasted_iota(jnp.int32, (tok, count), 1)
        row = lax.broadcasted_iota(jnp.int32, (tok, count), 0)
        scores = jnp.where(col <= row + j * tok, scores, -1e30)
        peak = jnp.max(scores, axis=1, keepdims=True)
        expo = jnp.exp(scores - peak)
        top[here] = jnp.broadcast_to(peak, (tok, DH))
        total[here] = jnp.broadcast_to(jnp.sum(expo, axis=1, keepdims=True), (tok, DH))
        accum[here] = jnp.dot(
            expo.astype(BF16), proj[:count, 2 * DH :], preferred_element_type=F32
        )

    def back_copy(j):
        return pltpu.make_async_remote_copy(
            src_ref=result.at[j], dst_ref=out.at[:, pl.ds(pl.multiple_of(pair * DH, DH), DH)],
            send_sem=send.at[j], recv_sem=recv.at[pair],
            device_id=(j * 2 + x, core), device_id_type=MESH,
        )

    for j in range(pairs):
        here = pl.ds(j * tok, tok)
        count = (j + 1) * tok
        if j * tok % rows == 0:
            kv_copy(j * tok // rows).wait_recv()
        scores = dot_t(proj[here, :DH], other[:count, :DH]) * scale
        col = lax.broadcasted_iota(jnp.int32, (tok, count), 1)
        scores = jnp.where(col < (j + x) * tok, scores, -1e30)
        peak = top[here]
        new_peak = jnp.maximum(peak, jnp.max(scores, axis=1, keepdims=True))
        factor = jnp.exp(peak - new_peak)
        expo = jnp.exp(scores - new_peak[:, :1])
        summed = total[here] * factor + jnp.sum(expo, axis=1, keepdims=True)
        value = accum[here] * factor + jnp.dot(
            expo.astype(BF16), other[:count, DH:], preferred_element_type=F32
        )
        result[j] = (value / summed).astype(BF16)

        @pl.when(j != pair)
        def _():
            back_copy(j).start()

    own = pltpu.make_async_copy(
        result.at[pair], out.at[:, pl.ds(pl.multiple_of(pair * DH, DH), DH)], local_sem
    )
    own.start()
    own.wait()
    for c in range(parts):
        kv_copy(c).wait_send()
    for j in range(pairs):

        @pl.when(j != pair)
        def _():
            back_copy(j).wait_send()

    for d in range(1, pairs):
        frm = (pair + d) % pairs
        pltpu.make_async_remote_copy(
            src_ref=result.at[frm],
            dst_ref=out.at[:, pl.ds(pl.multiple_of(frm * DH, DH), DH)],
            send_sem=send.at[frm], recv_sem=recv.at[frm],
            device_id=(frm * 2 + x, core), device_id_type=MESH,
        ).wait_recv()


def attend(projected, pairs, tok):
    vmem = pl.BlockSpec(memory_space=pltpu.VMEM)
    dma = pltpu.SemaphoreType.DMA
    rows = pairs * tok
    parts = 4
    return pl.pallas_call(
        functools.partial(attend_kernel, pairs, tok),
        out_shape=jax.ShapeDtypeStruct((tok, pairs * DH), BF16),
        in_specs=[vmem],
        out_specs=vmem,
        scratch_shapes=[
            pltpu.VMEM((rows, 2 * DH), BF16),
            pltpu.VMEM((rows, DH), F32),
            pltpu.VMEM((rows, DH), F32),
            pltpu.VMEM((rows, DH), F32),
            pltpu.VMEM((pairs, tok, DH), BF16),
            dma,
            dma((parts,)),
            dma((parts,)),
            dma((pairs,)),
            dma((pairs,)),
        ],
        compiler_params=pltpu.CompilerParams(
            collective_id=1, has_side_effects=True, vmem_limit_bytes=32 * 2**20
        ),
    )(projected)


def local_pairs(features, short_taps, long_filter, skip, norm_gain, w_qkv):
    ranks = lax.axis_size("ctx")
    pairs = ranks // 2
    me = lax.axis_index("ctx")
    core = lax.axis_index("tp")
    x = me % 2
    taps = short_taps.shape[0]
    tok = features.shape[2]
    width = features.shape[1] // ranks
    taps_here = lax.dynamic_slice_in_dim(short_taps, me * width, width, 2)
    skip_here = lax.dynamic_slice_in_dim(skip, me * width, width, 0)
    coef = jnp.concatenate([taps_here.reshape(taps * 3, width), skip_here[None]], axis=0).T
    coef = jnp.pad(coef, ((0, 0), (0, DH - coef.shape[1])))
    stacked = jnp.transpose(w_qkv, (1, 0, 2))
    gathered, w_all = hyena(features, long_filter, stacked, coef, ranks // 4, taps)
    channels = norm_gain.shape[0]
    whole = gathered.reshape(channels, pairs * tok)
    half = lax.dynamic_slice(
        gathered,
        (core, 0, 0, 0, (me // 2) * tok),
        (1, pairs, 2, width, tok),
    ).reshape(channels // 2, tok)
    whole_f = whole.astype(F32)
    inverse = lax.rsqrt(jnp.mean(whole_f * whole_f, axis=0, keepdims=True) + 1e-06)
    normed = (whole_f * inverse * norm_gain[:, None]).astype(BF16)
    projected = lax.dot_general(
        normed, w_all.reshape(channels, 3 * DH), (((0,), (0,)), ((), ())),
        preferred_element_type=F32,
    ).astype(BF16)
    attended = attend(projected, pairs, tok)
    return (half, attended)


def solution(mesh):
    in_specs = (
        P(None, "tp", "ctx"),
        P(None, None, "tp"),
        P("tp", "ctx"),
        P("tp"),
        P(),
        P("ctx", None, "tp"),
    )
    out_specs = (P("tp", "ctx"), P("ctx", "tp"))

    def whole(features, short_taps, long_filter, skip, norm_gain, w_qkv):
        heads = w_qkv.shape[2] // mesh.shape["tp"] // DH
        paired = mesh.shape["ctx"] == 16 and heads == 8
        body = local_pairs if paired else local
        return jax.shard_map(
            body, mesh=mesh, in_specs=in_specs, out_specs=out_specs, check_vma=False
        )(features, short_taps, long_filter, skip, norm_gain, w_qkv)

    return whole
```
